256 devices in a mesh: lat: 16 (over y, x_hi, core), lon: 16 (over x_lo, z).
Axes of the slice: x: 4 (x_hi: 2, x_lo: 2; x = x_hi * 2 + x_lo), y: 4, z: 8, core: 2. Of those that a mesh axis runs over, the one named last changes fastest.
Arguments:
- cotangent: bfloat16 [256, 1440, 512], P('lat', 'lon'), may hold values from -6 to 6
- activations: bfloat16 [256, 1440, 512], P('lat', 'lon'), may hold values from -6 to 6
- weight: bfloat16 [4, 512, 512], replicated, may hold values from -0.125 to 0.125
- basis: bfloat16 [4, 3, 33, 256], replicated, may hold values from -1.1953125 to 1.1953125
- reach: int32 [256], replicated, may hold values from 1 to 16, as said below
Outputs:
- grad_input: bfloat16 [256, 1440, 512], P('lat', 'lon')
- grad_weight: bfloat16 [4, 512, 512], replicated
The draws below stay inside these ranges and needn't reach their ends.
Inputs may be any that keep to these rules, and one draw needn't show every extreme that they name: reach of each latitude row, widest near the poles; rows 0 and 255 have reach 16.
All inputs are finite; a program needn't handle non-finite values.
Results may differ from the reference program's by a relative error of at most 0.0052.
Values may be sent and summed in bfloat16 or wider, within the bound.
No kernel may reach another device: no remote copies, remote signals or barrier semaphores. Data moves between devices by JAX's collectives and lax.ppermute only.
A program may use at most 128 MiB of HBM per device.

```python
import jax
import jax.numpy as jnp
from jax import lax

C = 512
K = 4
H = 16
R = 1
NLON = 1440
NLAT = 256


def draw_reach(key, part):
    key = jax.random.fold_in(key, 7)
    row_ids = jnp.arange(NLAT, dtype=jnp.int32)
    from_pole = jnp.minimum(row_ids, NLAT - 1 - row_ids)
    jitter = jax.random.randint(key, (NLAT,), 0, 3, dtype=jnp.int32)
    return jnp.minimum(H, 1 + 2 * H // (2 * from_pole + 1) + jitter).astype(jnp.int32)


def shard_levels(own_key, extent, cuts, smallest, top_value):
    factor_of, own = 1.0, jax.random.fold_in(own_key, 6)
    for dim, shards_of in cuts:
        heights = jnp.exp(jax.random.uniform(jax.random.fold_in(own, dim), (shards_of,), jnp.float32, smallest / len(cuts), top_value / len(cuts)))
        factor_of = factor_of * jnp.repeat(heights, extent[dim] // shards_of).reshape([-1 if axis == dim else 1 for axis in range(len(extent))])
    return factor_of


def scatter_about(stream_key, shape, deviation, most, cuts=(), kind=jnp.bfloat16):
    gain = shard_levels(stream_key, shape, cuts, -0.22, 0.18) if cuts else 1.0
    array = jax.random.normal(stream_key, shape, jnp.float32) * deviation * gain
    return jnp.minimum(jnp.maximum(array, -most), most).astype(kind)


def setup_inputs(seed: int = 0) -> dict:
    seeds = jax.random.split(jax.random.key(seed), 6)
    cotangent = scatter_about(seeds[0], (NLAT, NLON, C), 1.0, 6.0, ((0, 16), (1, 16)))
    activations = scatter_about(seeds[1], (NLAT, NLON, C), 1.0, 6.0, ((0, 16), (1, 16)))
    weight = scatter_about(seeds[2], (K, C, C), (K * C) ** -0.5, 0.125)
    basis = scatter_about(seeds[3], (K, 2 * R + 1, 2 * H + 1, NLAT), 0.2, 1.1953125)
    reach = draw_reach(jax.random.fold_in(seeds[5], 71), 0)
    return {"cotangent": cotangent, "activations": activations, "weight": weight, "basis": basis, "reach": reach}


def transposed_stencil(cot_block, tap_table):
    group_size = cot_block.shape[2]
    widened = jnp.zeros((NLAT + 2 * R, NLON, group_size), jnp.float32)
    for tap_row in range(2 * R + 1):
        row_taps = tap_table[tap_row]

        def add_offset(carried, tap_col):
            moved = jnp.roll(cot_block, tap_col - H, axis=1)
            weights_col = lax.dynamic_index_in_dim(row_taps, tap_col, 0, keepdims=False)
            return carried + weights_col[:, None, None] * moved, None

        placed, _ = lax.scan(add_offset, jnp.zeros_like(cot_block), jnp.arange(2 * H + 1, dtype=jnp.int32))
        widened = widened.at[tap_row:tap_row + NLAT].add(placed)
    folded = widened[R:R + NLAT]
    for polar_row in range(R):
        folded = folded.at[polar_row].add(jnp.roll(widened[R - 1 - polar_row], NLON // 2, axis=0))
        folded = folded.at[NLAT - 1 - polar_row].add(jnp.roll(widened[R + NLAT + polar_row], NLON // 2, axis=0))
    return folded


def reference(cotangent, activations, weight, basis, reach):
    offsets = jnp.arange(2 * H + 1, dtype=jnp.int32) - H
    inside = (jnp.abs(offsets)[:, None] <= reach[None, :]).astype(jnp.float32)
    tap_table = basis.astype(jnp.float32) * inside[None, None, :, :]
    group_size = min(C, 64)
    blocks = C // group_size
    cell_count = NLAT * NLON
    input_flat = activations.reshape(cell_count, C)

    def one_block(carried, step_index):
        filter_index = step_index // blocks
        block_start = (step_index % blocks) * group_size
        cot_block = lax.dynamic_slice_in_dim(cotangent, block_start, group_size, 2).astype(jnp.float32)
        filter_taps = lax.dynamic_index_in_dim(tap_table, filter_index, 0, keepdims=False)
        filter_block = transposed_stencil(cot_block, filter_taps).astype(jnp.bfloat16).reshape(cell_count, group_size)
        weight_rows = lax.dynamic_slice_in_dim(lax.dynamic_index_in_dim(weight, filter_index, 0, keepdims=False), block_start, group_size, 0)
        carried = carried + jnp.dot(filter_block, weight_rows, preferred_element_type=jnp.float32)
        return carried, jnp.dot(filter_block.T, input_flat, preferred_element_type=jnp.float32)

    grad_sum, pieces = lax.scan(one_block, jnp.zeros((cell_count, C), jnp.float32), jnp.arange(K * blocks, dtype=jnp.int32))
    grad_input = grad_sum.reshape(NLAT, NLON, C).astype(jnp.bfloat16)
    grad_weight = (pieces.reshape(K, C, C) * (float(cell_count) ** -0.5)).astype(jnp.bfloat16)
    return grad_input, grad_weight
```

```python
import functools

import jax
import jax.numpy as jnp
from jax import lax
from jax.experimental import pallas as pl
from jax.experimental.pallas import tpu as pltpu
from jax.sharding import Mesh, PartitionSpec as P

ROWS, COLS, WIDE, PAD, REACH = 16, 90, 128, 96, 16
GAP = WIDE - COLS - 2 * REACH
RIGHT = WIDE - REACH
CHANNELS, FILTERS, TAPS = 512, 4, 3
AXES = ("y", "xh", "core", "xl", "z")
CHIPS = ("y", "xh", "xl", "z")
LAT, LON = 16, 16
VMEM = 60 * 1024 * 1024


def tiles_kernel(rev_ref, out_ref):
    lane = lax.broadcasted_iota(jnp.int32, (32, WIDE), 1)
    row = lax.broadcasted_iota(jnp.int32, (32, WIDE), 0) + 64
    for q in range(TAPS):
        for k in range(FILTERS):
            taps = rev_ref[0, pl.ds(q * FILTERS + k, 1), :]
            top = pltpu.roll(jnp.broadcast_to(taps, (64, WIDE)), 0, 1, stride=1, stride_axis=0)
            low = jnp.broadcast_to(taps, (32, WIDE))
            main = pltpu.roll(low, 64, 1, stride=1, stride_axis=0)
            right = pltpu.roll(low, 64 + GAP, 1, stride=1, stride_axis=0)
            low = jnp.where(lane < REACH + COLS, main, jnp.where(lane >= RIGHT, right, 0.0))
            low = jnp.where(row < COLS, low, 0.0)
            out_ref[0, k * PAD : k * PAD + 64, q * WIDE : (q + 1) * WIDE] = top.astype(jnp.bfloat16)
            out_ref[0, k * PAD + 64 : (k + 1) * PAD, q * WIDE : (q + 1) * WIDE] = low.astype(jnp.bfloat16)


def band_tiles(rev):
    return pl.pallas_call(
        tiles_kernel,
        grid=(ROWS,),
        in_specs=[pl.BlockSpec((1, 16, WIDE), lambda i: (i, 0, 0))],
        out_specs=pl.BlockSpec((1, FILTERS * PAD, TAPS * WIDE), lambda i: (i, 0, 0)),
        out_shape=jax.ShapeDtypeStruct((ROWS, FILTERS * PAD, TAPS * WIDE), jnp.bfloat16),
        name="band_tiles",
    )(rev)


def pad_rows(scratch, start, block):
    scratch[pl.ds(start + 80, 16), :] = jnp.zeros((16, CHANNELS), jnp.bfloat16)
    scratch[pl.ds(start, COLS), :] = block


def stencil_kernel(core, tiles, own, left, right, before, after, act, f_out, send, source, held, cells):
    step = pl.program_id(0)

    @pl.when(step == 0)
    def _():
        source[pl.ds(0, WIDE), :] = before[0]
        source[pl.ds((ROWS + 1) * WIDE, WIDE), :] = after[0]
        for r in range(ROWS):
            base = (r + 1) * WIDE
            source[pl.ds(base, REACH), :] = left[r]
            pad_rows(source, base + REACH, own[r])
            source[pl.ds(base + RIGHT, REACH), :] = right[r]
            pad_rows(cells, r * PAD, act[r])

    @pl.when(step < ROWS)
    def _():
        rows = source[pl.ds(pl.multiple_of(step * WIDE, WIDE), TAPS * WIDE), :]
        f = jnp.dot(tiles[0], rows, preferred_element_type=jnp.float32).astype(jnp.bfloat16)
        for k in range(FILTERS):
            part = f[k * PAD : (k + 1) * PAD]
            f_out[k] = part
            held[k, pl.ds(pl.multiple_of(step * PAD, 32), PAD), :] = part

    @pl.when(step >= ROWS)
    def _():
        k = 2 * (1 - core[0]) + step - ROWS
        d = lax.dot_general(held[k], cells[...], (((0,), (0,)), ((), ())), preferred_element_type=jnp.float32)
        send[0] = d.astype(jnp.bfloat16)


def stencil(core, tiles, own, left, right, before, after, act):
    whole = lambda a: pl.BlockSpec(a.shape, lambda i, c: (0,) * a.ndim)
    return pl.pallas_call(
        stencil_kernel,
        grid_spec=pltpu.PrefetchScalarGridSpec(
            num_scalar_prefetch=1,
            grid=(ROWS + 2,),
            in_specs=[
                pl.BlockSpec((1, FILTERS * PAD, TAPS * WIDE), lambda i, c: (jnp.minimum(i, ROWS - 1), 0, 0)),
                whole(own), whole(left), whole(right), whole(before), whole(after), whole(act),
            ],
            out_specs=[
                pl.BlockSpec((FILTERS, PAD, CHANNELS), lambda i, c: (0, jnp.minimum(i, ROWS - 1), 0)),
                pl.BlockSpec((1, CHANNELS, CHANNELS), lambda i, c: (jnp.maximum(i - ROWS, 0), 0, 0)),
            ],
            scratch_shapes=[
                pltpu.VMEM(((ROWS + 2) * WIDE, CHANNELS), jnp.bfloat16),
                pltpu.VMEM((FILTERS, ROWS * PAD, CHANNELS), jnp.bfloat16),
                pltpu.VMEM((ROWS * PAD, CHANNELS), jnp.bfloat16),
            ],
        ),
        out_shape=[
            jax.ShapeDtypeStruct((FILTERS, ROWS * PAD, CHANNELS), jnp.bfloat16),
            jax.ShapeDtypeStruct((2, CHANNELS, CHANNELS), jnp.bfloat16),
        ],
        compiler_params=pltpu.CompilerParams(vmem_limit_bytes=VMEM),
        name="stencil",
    )(core, tiles, own, left, right, before, after, act)


def input_kernel(f, weight, out):
    total = jnp.dot(f[0], weight[0], preferred_element_type=jnp.float32)
    for k in range(1, FILTERS):
        total += jnp.dot(f[k], weight[k], preferred_element_type=jnp.float32)
    for r in range(out.shape[0]):
        out[r] = total[r * PAD : r * PAD + COLS].astype(jnp.bfloat16)


def input_gradient(f, weight):
    group = 4
    flops = 2 * ROWS * PAD * FILTERS * CHANNELS * CHANNELS
    return pl.pallas_call(
        input_kernel,
        grid=(ROWS // group,),
        in_specs=[
            pl.BlockSpec((FILTERS, group * PAD, CHANNELS), lambda i: (0, i, 0)),
            pl.BlockSpec((FILTERS, CHANNELS, CHANNELS), lambda i: (0, 0, 0)),
        ],
        out_specs=pl.BlockSpec((group, COLS, CHANNELS), lambda i: (i, 0, 0)),
        out_shape=jax.ShapeDtypeStruct((ROWS, COLS, CHANNELS), jnp.bfloat16),
        compiler_params=pltpu.CompilerParams(vmem_limit_bytes=VMEM),
        cost_estimate=pl.CostEstimate(flops=flops, bytes_accessed=10_000_000, transcendentals=0),
        name="input_gradient",
    )(f, weight)


def own_half_kernel(core, f, act, got, out, cells):
    @pl.when(pl.program_id(0) == 0)
    def _():
        for r in range(ROWS):
            pad_rows(cells, r * PAD, act[r])

    d = lax.dot_general(f[0], cells[...], (((0,), (0,)), ((), ())), preferred_element_type=jnp.float32)
    out[0] = (d + got[0].astype(jnp.float32)).astype(jnp.bfloat16)


def own_half(core, f, act, got):
    block = (1, CHANNELS, CHANNELS)
    return pl.pallas_call(
        own_half_kernel,
        grid_spec=pltpu.PrefetchScalarGridSpec(
            num_scalar_prefetch=1,
            grid=(2,),
            in_specs=[
                pl.BlockSpec((1, ROWS * PAD, CHANNELS), lambda i, c: (2 * c[0] + i, 0, 0)),
                pl.BlockSpec(act.shape, lambda i, c: (0, 0, 0)),
                pl.BlockSpec(block, lambda i, c: (i, 0, 0)),
            ],
            out_specs=pl.BlockSpec(block, lambda i, c: (i, 0, 0)),
            scratch_shapes=[pltpu.VMEM((ROWS * PAD, CHANNELS), jnp.bfloat16)],
        ),
        out_shape=jax.ShapeDtypeStruct((2, CHANNELS, CHANNELS), jnp.bfloat16),
        compiler_params=pltpu.CompilerParams(vmem_limit_bytes=VMEM),
        name="own_half",
    )(core, f, act, got)


def device(lat, lon):
    return (lat % LAT) * LON + lon % LON


def route(pairs):
    return [(device(*a), device(*b)) for a, b in pairs]


GRID = [(a, b) for a in range(LAT) for b in range(LON)]
EAST = route(((a, b), (a, b + 1)) for a, b in GRID)
WEST = route(((a, b), (a, b - 1)) for a, b in GRID)
SOUTH = route(((a, b), (a + 1, b)) for a, b in GRID if a < LAT - 1)
NORTH = route(((a, b), (a - 1, b)) for a, b in GRID if a > 0)
ACROSS = route(((a, b), (a, b + LON // 2)) for a, b in GRID if a in (0, LAT - 1))
SIBLING = route(((a, b), (a ^ 1, b)) for a, b in GRID)


def reversed_taps(basis, reach, band):
    span = basis.shape[2]
    offsets = jnp.arange(span, dtype=jnp.int32) - REACH
    masked = jnp.where(jnp.abs(offsets)[:, None] <= reach[None, :], basis, 0)
    total = masked.shape[3]
    slabs = []
    for q in range(TAPS):
        t = TAPS - 1 - q
        edge = jnp.zeros_like(masked[:, t, :, :1])
        first = masked[:, 0, :, :1] if q == 0 else edge
        last = masked[:, 2, :, total - 1 :] if q == 2 else edge
        padded = jnp.concatenate([first, masked[:, t], last], axis=2)
        slabs.append(lax.dynamic_slice_in_dim(padded, band * ROWS + q, ROWS, 2))
    taps = jnp.stack(slabs)[:, :, ::-1, :].astype(jnp.float32)
    taps = jnp.transpose(taps, (3, 0, 1, 2)).reshape(ROWS, TAPS * FILTERS, span)
    return jnp.pad(taps, ((0, 0), (0, 16 - TAPS * FILTERS), (0, WIDE - span)))


def on_device(cotangent, activations, weight, basis, reach):
    band = lax.axis_index(("y", "xh", "core"))
    core = lax.axis_index("core").astype(jnp.int32)
    cores = core[None]
    left = lax.ppermute(cotangent[:, COLS - REACH :], AXES, EAST)
    right = lax.ppermute(cotangent[:, :REACH], AXES, WEST)
    tiles = band_tiles(reversed_taps(basis, reach, band))
    zeros = jnp.zeros((1, GAP, CHANNELS), jnp.bfloat16)
    first, last = (
        jnp.concatenate([left[r : r + 1], cotangent[r : r + 1], zeros, right[r : r + 1]], axis=1) for r in (0, ROWS - 1)
    )
    before = lax.ppermute(last, AXES, SOUTH)
    after = lax.ppermute(first, AXES, NORTH)
    mirror = lax.ppermute(jnp.where(band == 0, first, last), AXES, ACROSS)
    before = jnp.where(band == 0, mirror, before)
    after = jnp.where(band == LAT - 1, mirror, after)
    f, send = stencil(cores, tiles, cotangent, left, right, before, after, activations)
    got = lax.ppermute(send, AXES, SIBLING)
    grad_input = input_gradient(f, weight)
    half = own_half(cores, f, activations, got)
    chips = LAT * LON // 2
    parts = half.reshape(chips, 2 * CHANNELS // chips, CHANNELS)
    parts = lax.all_to_all(parts, CHIPS, 0, 0, tiled=True)
    norm_factor = float(ROWS * COLS * LAT * LON) ** (-0.5)
    part = (jnp.sum(parts.astype(jnp.float32), axis=0) * norm_factor).astype(jnp.bfloat16)
    parts = lax.all_to_all(jnp.broadcast_to(part, parts.shape), CHIPS, 0, 0, tiled=True)
    mine = parts.reshape(2, CHANNELS, CHANNELS)
    theirs = lax.ppermute(mine, AXES, SIBLING)
    grad_weight = jnp.where(core == 0, jnp.concatenate([mine, theirs]), jnp.concatenate([theirs, mine]))
    return grad_input, grad_weight


def solution(mesh):
    finer = Mesh(mesh.devices.reshape(4, 2, 2, 2, 8), AXES)
    cells = P(("y", "xh", "core"), ("xl", "z"), None)
    return jax.shard_map(
        on_device, mesh=finer, in_specs=(cells, cells, P(), P(), P()), out_specs=(cells, P()), check_vma=False
    )
```

```python
import jax
import jax.numpy as jnp
from jax import lax
from jax.experimental import pallas as pl
from jax.experimental.pallas import tpu as pltpu
from jax.sharding import Mesh, PartitionSpec as P

ROWS, COLS, REACH = 16, 90, 16
PAD, HALF, SPAN, WIDE = 96, 48, 80, 128
DEPTH = 256
CHANNELS, FILTERS, TAPS = 512, 4, 3
AXES = ("y", "xh", "core", "xl", "zh", "zl")
BLOCK = ("y", "xh", "xl", "zl")
LAT, LON = 16, 16
VMEM = 56 * 1024 * 1024
BF16, F32 = jnp.bfloat16, jnp.float32


def turned(block):
    return jnp.swapaxes(block, 0, 1)


def prepare_kernel(taps, act, tiles, cells):
    step = pl.program_id(0)
    for r in range(ROWS // 2):
        for k in range(FILTERS):
            row = jnp.broadcast_to(taps[r, pl.ds(k, 1), :], (HALF, DEPTH))
            band = pltpu.roll(row, 0, 1, stride=1, stride_axis=0)
            tiles[r, k * HALF : (k + 1) * HALF, :] = band.astype(BF16)
    col = lax.broadcasted_iota(jnp.int32, (16, 16, CHANNELS), 0)
    for b in range(HALF // 16):
        block = act[b * 16 : (b + 1) * 16]
        if (b + 1) * 16 > COLS - HALF:
            block = jnp.where(col + (step * HALF + b * 16) < COLS, block, jnp.zeros_like(block))
        cells[:, b * 16 : (b + 1) * 16, :] = turned(block)


def prepare(taps, act):
    return pl.pallas_call(
        prepare_kernel,
        grid=(2,),
        in_specs=[
            pl.BlockSpec((ROWS // 2, 8, DEPTH), lambda i: (i, 0, 0)),
            pl.BlockSpec((HALF, ROWS, CHANNELS), lambda i: (i, 0, 0)),
        ],
        out_specs=[
            pl.BlockSpec((ROWS // 2, FILTERS * HALF, DEPTH), lambda i: (i, 0, 0)),
            pl.BlockSpec((ROWS, HALF, CHANNELS), lambda i: (0, i, 0)),
        ],
        out_shape=[
            jax.ShapeDtypeStruct((ROWS, FILTERS * HALF, DEPTH), BF16),
            jax.ShapeDtypeStruct((ROWS, PAD, CHANNELS), BF16),
        ],
        cost_estimate=pl.CostEstimate(flops=10_000_000, bytes_accessed=5_000_000, transcendentals=0),
        compiler_params=pltpu.CompilerParams(vmem_limit_bytes=VMEM),
        name="prepare",
    )(taps, act)


GROUP = 4
STEPS = ROWS // GROUP


def outer(f, cells):
    f = f.reshape(ROWS * PAD, CHANNELS)
    cells = cells.reshape(ROWS * PAD, CHANNELS)
    return lax.dot_general(f, cells, (((0,), (0,)), ((), ())), preferred_element_type=F32)


def stencil_kernel(place, tiles, own, lon_a, lon_b, lat_a, lat_b, cells, f_out, send, low, high, held):
    step = pl.program_id(0)

    @pl.when(step == 0)
    def _():
        even = place[1] == 0
        left = jnp.where(even, lon_b[...], lon_a[...])
        right = jnp.where(even, lon_a[...], lon_b[...])
        blocks = [left] + [own[16 * b : 16 * (b + 1)] for b in range(5)]
        blocks.append(jnp.concatenate([own[80:COLS], right[:6]]))
        blocks.append(jnp.concatenate([right[6:], jnp.zeros((6, ROWS, CHANNELS), BF16)]))
        for b, block in enumerate(blocks):
            block = turned(block)
            if b < 5:
                low[1 : ROWS + 1, 16 * b : 16 * (b + 1), :] = block
            if b > 2:
                high[1 : ROWS + 1, 16 * (b - 3) : 16 * (b - 2), :] = block
        first = place[0] == 0
        before = jnp.where(first, lat_b[...], lat_a[...])
        after = jnp.where(first, lat_a[...], lat_b[...])
        low[0], low[ROWS + 1] = before[:SPAN], after[:SPAN]
        high[0], high[ROWS + 1] = before[HALF:], after[HALF:]

    @pl.when(step < STEPS)
    def _():
        rest = jnp.zeros((DEPTH - TAPS * SPAN, CHANNELS), BF16)
        for j in range(GROUP):
            r = step * GROUP + j
            for h, source in enumerate((low, high)):
                rows = source[pl.ds(r, TAPS)].reshape(TAPS * SPAN, CHANNELS)
                rows = jnp.concatenate([rows, rest])
                f = jnp.dot(tiles[j], rows, preferred_element_type=F32).astype(BF16)
                f = f.reshape(FILTERS, HALF, CHANNELS)
                f_out[:, j, h * HALF : (h + 1) * HALF, :] = f
                held[:, r, h * HALF : (h + 1) * HALF, :] = f

    @pl.when(step >= STEPS)
    def _():
        k = 2 * (1 - place[0]) + step - STEPS
        send[0] = outer(held[k], cells[...]).astype(BF16)


def stencil(place, tiles, own, lon_a, lon_b, lat_a, lat_b, cells):
    whole = lambda a: pl.BlockSpec(a.shape, lambda i, c: (0,) * a.ndim)
    return pl.pallas_call(
        stencil_kernel,
        grid_spec=pltpu.PrefetchScalarGridSpec(
            num_scalar_prefetch=1,
            grid=(STEPS + 2,),
            in_specs=[
                pl.BlockSpec((GROUP, FILTERS * HALF, DEPTH), lambda i, c: (jnp.minimum(i, STEPS - 1), 0, 0)),
                *[whole(a) for a in (own, lon_a, lon_b, lat_a, lat_b, cells)],
            ],
            out_specs=[
                pl.BlockSpec((FILTERS, GROUP, PAD, CHANNELS), lambda i, c: (0, jnp.minimum(i, STEPS - 1), 0, 0)),
                pl.BlockSpec((1, CHANNELS, CHANNELS), lambda i, c: (jnp.maximum(i - STEPS, 0), 0, 0)),
            ],
            scratch_shapes=[
                pltpu.VMEM((ROWS + 2, SPAN, CHANNELS), BF16),
                pltpu.VMEM((ROWS + 2, SPAN, CHANNELS), BF16),
                pltpu.VMEM((FILTERS, ROWS, PAD, CHANNELS), BF16),
            ],
        ),
        out_shape=[
            jax.ShapeDtypeStruct((FILTERS, ROWS, PAD, CHANNELS), BF16),
            jax.ShapeDtypeStruct((2, CHANNELS, CHANNELS), BF16),
        ],
        compiler_params=pltpu.CompilerParams(vmem_limit_bytes=VMEM),
        name="stencil",
    )(place, tiles, own, lon_a, lon_b, lat_a, lat_b, cells)


def input_kernel(f, weight, out):
    cols = out.shape[0]
    total = 0.0
    for k in range(FILTERS):
        total += jnp.dot(f[k].reshape(ROWS * cols, CHANNELS), weight[k], preferred_element_type=F32)
    total = total.astype(BF16).reshape(ROWS, cols, CHANNELS)
    for b in range(cols // 16):
        out[b * 16 : (b + 1) * 16] = turned(total[:, b * 16 : (b + 1) * 16])


def input_gradient(f, weight):
    cols = 32
    flops = 2 * ROWS * PAD * FILTERS * CHANNELS * CHANNELS
    return pl.pallas_call(
        input_kernel,
        grid=(PAD // cols,),
        in_specs=[
            pl.BlockSpec((FILTERS, ROWS, cols, CHANNELS), lambda i: (0, 0, i, 0)),
            pl.BlockSpec((FILTERS, CHANNELS, CHANNELS), lambda i: (0, 0, 0)),
        ],
        out_specs=pl.BlockSpec((cols, ROWS, CHANNELS), lambda i: (i, 0, 0)),
        out_shape=jax.ShapeDtypeStruct((COLS, ROWS, CHANNELS), BF16),
        compiler_params=pltpu.CompilerParams(vmem_limit_bytes=VMEM),
        cost_estimate=pl.CostEstimate(flops=flops, bytes_accessed=10_000_000, transcendentals=0),
        name="input_gradient",
    )(f, weight)


def own_half_kernel(place, f, cells, got, out):
    out[0] = (outer(f[0], cells[...]) + got[0].astype(F32)).astype(BF16)


def own_half(place, f, cells, got):
    block = (1, CHANNELS, CHANNELS)
    return pl.pallas_call(
        own_half_kernel,
        grid_spec=pltpu.PrefetchScalarGridSpec(
            num_scalar_prefetch=1,
            grid=(2,),
            in_specs=[
                pl.BlockSpec((1, ROWS, PAD, CHANNELS), lambda i, c: (2 * c[0] + i, 0, 0, 0)),
                pl.BlockSpec(cells.shape, lambda i, c: (0, 0, 0)),
                pl.BlockSpec(block, lambda i, c: (i, 0, 0)),
            ],
            out_specs=pl.BlockSpec(block, lambda i, c: (i, 0, 0)),
        ),
        out_shape=jax.ShapeDtypeStruct((2, CHANNELS, CHANNELS), BF16),
        compiler_params=pltpu.CompilerParams(vmem_limit_bytes=VMEM),
        name="own_half",
    )(place, f, cells, got)


def device(lat, lon):
    return lat * LON + lon % LON


def route(target):
    return [(device(a, b), device(*target(a, b))) for a in range(LAT) for b in range(LON)]


def lat_b_partner(a, b):
    if a in (0, LAT - 1):
        return a, b + LON // 2
    return (a + 1 if a % 2 else a - 1), b


LON_A = route(lambda a, b: (a, b ^ 1))
LON_B = route(lambda a, b: (a, b + 1 if b % 2 else b - 1))
LAT_A = route(lambda a, b: (a ^ 1, b))
LAT_B = route(lat_b_partner)
SIBLING = LAT_A


def along_z(mask):
    return route(lambda a, b: (a, b ^ mask))


def reversed_taps(basis, reach, band):
    span = basis.shape[2]
    offsets = jnp.arange(span, dtype=jnp.int32) - REACH
    masked = jnp.where(jnp.abs(offsets)[:, None] <= reach[None, :], basis, 0)
    total = masked.shape[3]
    slabs = []
    for q in range(TAPS):
        t = TAPS - 1 - q
        edge = jnp.zeros_like(masked[:, t, :, :1])
        first = masked[:, 0, :, :1] if q == 0 else edge
        last = masked[:, 2, :, total - 1 :] if q == 2 else edge
        padded = jnp.concatenate([first, masked[:, t], last], axis=2)
        slabs.append(lax.dynamic_slice_in_dim(padded, band * ROWS + q, ROWS, 2))
    taps = jnp.stack(slabs)[:, :, ::-1, :].astype(F32)
    taps = jnp.pad(jnp.transpose(taps, (3, 1, 0, 2)), ((0, 0), (0, 0), (0, 0), (0, SPAN - span)))
    taps = taps.reshape(ROWS, FILTERS, TAPS * SPAN)
    return jnp.pad(taps, ((0, 0), (0, 8 - FILTERS), (0, DEPTH - TAPS * SPAN)))


def haloes(own, core, odd):
    start_a = jnp.where(odd == 0, COLS - REACH, 0)
    start_b = jnp.where(odd == 0, 0, COLS - REACH)
    lon_a, lon_b = (lax.dynamic_slice_in_dim(own, s, REACH, 0) for s in (start_a, start_b))
    row_a = jnp.where(core == 0, ROWS - 1, 0)
    row_b = ROWS - 1 - row_a
    edges = lambda x: jnp.concatenate([x[:, :1], x[:, ROWS - 1 :]], axis=1)
    edge_a = lax.ppermute(edges(lon_a), AXES, LON_A)
    edge_b = lax.ppermute(edges(lon_b), AXES, LON_B)
    lon_a = lax.ppermute(lon_a, AXES, LON_A)
    lon_b = lax.ppermute(lon_b, AXES, LON_B)
    left = jnp.where(odd == 0, edge_b, edge_a)
    right = jnp.where(odd == 0, edge_a, edge_b)
    middle = edges(own)
    rest = jnp.zeros((WIDE - COLS - 2 * REACH, 2, CHANNELS), BF16)
    wide = jnp.concatenate([left, middle, right, rest])
    first, last = wide[:, 0], wide[:, 1]
    lat_a = lax.ppermute(jnp.where(core == 0, last, first), AXES, LAT_A)
    lat_b = lax.ppermute(jnp.where(core == 0, first, last), AXES, LAT_B)
    return lon_a, lon_b, lat_a, lat_b


def summed(parts, groups, axes):
    parts = lax.all_to_all(parts.reshape(groups, -1, CHANNELS), axes, 0, 0, tiled=True)
    return jnp.sum(parts.astype(F32), axis=0)


def on_device(cotangent, activations, weight, basis, reach):
    band = lax.axis_index(("y", "xh", "core"))
    core = lax.axis_index("core").astype(jnp.int32)
    odd = lax.axis_index("zl").astype(jnp.int32)
    place = jnp.stack([core, odd])
    own, act = jnp.swapaxes(cotangent, 0, 1), jnp.swapaxes(activations, 0, 1)
    around = haloes(own, core, odd)
    tiles, cells = prepare(reversed_taps(basis, reach, band), act)
    f, send = stencil(place, tiles, own, *around, cells)
    got = lax.ppermute(send, AXES, SIBLING)
    grad_input = jnp.swapaxes(input_gradient(f, weight), 0, 1)
    half = own_half(place, f, cells, got)
    part = lax.optimization_barrier(summed(half.reshape(-1, CHANNELS), 32, BLOCK).astype(BF16))
    others = [lax.ppermute(part, AXES, along_z(m)).astype(F32) for m in (2, 6, 4)]
    norm_factor = float(ROWS * COLS * LAT * LON) ** (-0.5)
    part = (part.astype(F32) + others[0]) + (others[1] + others[2])
    part = (part * norm_factor).astype(BF16)
    parts = lax.all_to_all(jnp.broadcast_to(part, (32, *part.shape)), BLOCK, 0, 0, tiled=True)
    mine = parts.reshape(2, CHANNELS, CHANNELS)
    theirs = lax.ppermute(mine, AXES, SIBLING)
    grad_weight = jnp.where(core == 0, jnp.concatenate([mine, theirs]), jnp.concatenate([theirs, mine]))
    return grad_input, grad_weight


def solution(mesh):
    finer = Mesh(mesh.devices.reshape(4, 2, 2, 2, 4, 2), AXES)
    cells = P(("y", "xh", "core"), ("xl", "zh", "zl"), None)
    return jax.shard_map(
        on_device, mesh=finer, in_specs=(cells, cells, P(), P(), P()), out_specs=(cells, P()), check_vma=False
    )
```

```python
import jax
import jax.numpy as jnp
from jax import lax
from jax.experimental import pallas as pl
from jax.experimental.pallas import tpu as pltpu
from jax.sharding import Mesh, PartitionSpec as P

ROWS, COLS, REACH = 16, 90, 16
PAD, HALF, SPAN, WIDE = 96, 48, 80, 128
DEPTH = 256
CHANNELS, FILTERS, TAPS = 512, 4, 3
AXES = ("y", "xh", "core", "xl", "zh", "zl")
BLOCK = ("y", "xh", "xl", "zl")
LAT, LON = 16, 16
MIB = 1024 * 1024
BF16, F32 = jnp.bfloat16, jnp.float32


def turned(block):
    return jnp.swapaxes(block, 0, 1)


def prepare_kernel(taps, act, tiles, cells):
    step = pl.program_id(0)
    for r in range(ROWS // 2):
        for k in range(FILTERS):
            row = jnp.broadcast_to(taps[r, pl.ds(k, 1), :], (HALF, DEPTH))
            band = pltpu.roll(row, 0, 1, stride=1, stride_axis=0)
            tiles[r, k * HALF : (k + 1) * HALF, :] = band.astype(BF16)
    col = lax.broadcasted_iota(jnp.int32, (16, 16, CHANNELS), 0)
    for b in range(HALF // 16):
        block = act[b * 16 : (b + 1) * 16]
        if (b + 1) * 16 > COLS - HALF:
            block = jnp.where(col + (step * HALF + b * 16) < COLS, block, jnp.zeros_like(block))
        cells[:, b * 16 : (b + 1) * 16, :] = turned(block)


def prepare(taps, act):
    return pl.pallas_call(
        prepare_kernel,
        grid=(2,),
        in_specs=[
            pl.BlockSpec((ROWS // 2, 8, DEPTH), lambda i: (i, 0, 0)),
            pl.BlockSpec((HALF, ROWS, CHANNELS), lambda i: (i, 0, 0)),
        ],
        out_specs=[
            pl.BlockSpec((ROWS // 2, FILTERS * HALF, DEPTH), lambda i: (i, 0, 0)),
            pl.BlockSpec((ROWS, HALF, CHANNELS), lambda i: (0, i, 0)),
        ],
        out_shape=[
            jax.ShapeDtypeStruct((ROWS, FILTERS * HALF, DEPTH), BF16),
            jax.ShapeDtypeStruct((ROWS, PAD, CHANNELS), BF16),
        ],
        cost_estimate=pl.CostEstimate(flops=10_000_000, bytes_accessed=5_000_000, transcendentals=0),
        compiler_params=pltpu.CompilerParams(vmem_limit_bytes=16 * MIB),
        name="prepare",
    )(taps, act)


GROUP = 4
STEPS = ROWS // GROUP


def outer(f, cells):
    f = f.reshape(ROWS * PAD, CHANNELS)
    cells = cells.reshape(ROWS * PAD, CHANNELS)
    return lax.dot_general(f, cells, (((0,), (0,)), ((), ())), preferred_element_type=F32)


def stencil_kernel(place, tiles, own, lon_a, lon_b, lat_a, lat_b, cells, f_out, send, low, high, held):
    step = pl.program_id(0)

    @pl.when(step == 0)
    def _():
        even = place[1] == 0
        left = jnp.where(even, lon_b[...], lon_a[...])
        right = jnp.where(even, lon_a[...], lon_b[...])
        blocks = [left] + [own[16 * b : 16 * (b + 1)] for b in range(5)]
        blocks.append(jnp.concatenate([own[80:COLS], right[:6]]))
        blocks.append(jnp.concatenate([right[6:], jnp.zeros((6, ROWS, CHANNELS), BF16)]))
        for b, block in enumerate(blocks):
            block = turned(block)
            if b < 5:
                low[1 : ROWS + 1, 16 * b : 16 * (b + 1), :] = block
            if b > 2:
                high[1 : ROWS + 1, 16 * (b - 3) : 16 * (b - 2), :] = block
        first = place[0] == 0
        before = jnp.where(first, lat_b[...], lat_a[...])
        after = jnp.where(first, lat_a[...], lat_b[...])
        low[0], low[ROWS + 1] = before[:SPAN], after[:SPAN]
        high[0], high[ROWS + 1] = before[HALF:], after[HALF:]

    @pl.when(step < STEPS)
    def _():
        rest = jnp.zeros((DEPTH - TAPS * SPAN, CHANNELS), BF16)
        for j in range(GROUP):
            r = step * GROUP + j
            for h, source in enumerate((low, high)):
                rows = source[pl.ds(r, TAPS)].reshape(TAPS * SPAN, CHANNELS)
                rows = jnp.concatenate([rows, rest])
                f = jnp.dot(tiles[j], rows, preferred_element_type=F32).astype(BF16)
                f = f.reshape(FILTERS, HALF, CHANNELS)
                f_out[:, j, h * HALF : (h + 1) * HALF, :] = f
                held[:, r, h * HALF : (h + 1) * HALF, :] = f

    @pl.when(step >= STEPS)
    def _():
        k = 2 * (1 - place[0]) + step - STEPS
        send[0] = outer(held[k], cells[...]).astype(BF16)


def stencil(place, tiles, own, lon_a, lon_b, lat_a, lat_b, cells):
    whole = lambda a: pl.BlockSpec(a.shape, lambda i, c: (0,) * a.ndim)
    return pl.pallas_call(
        stencil_kernel,
        grid_spec=pltpu.PrefetchScalarGridSpec(
            num_scalar_prefetch=1,
            grid=(STEPS + 2,),
            in_specs=[
                pl.BlockSpec((GROUP, FILTERS * HALF, DEPTH), lambda i, c: (jnp.minimum(i, STEPS - 1), 0, 0)),
                *[whole(a) for a in (own, lon_a, lon_b, lat_a, lat_b, cells)],
            ],
            out_specs=[
                pl.BlockSpec((FILTERS, GROUP, PAD, CHANNELS), lambda i, c: (0, jnp.minimum(i, STEPS - 1), 0, 0)),
                pl.BlockSpec((1, CHANNELS, CHANNELS), lambda i, c: (jnp.maximum(i - STEPS, 0), 0, 0)),
            ],
            scratch_shapes=[
                pltpu.VMEM((ROWS + 2, SPAN, CHANNELS), BF16),
                pltpu.VMEM((ROWS + 2, SPAN, CHANNELS), BF16),
                pltpu.VMEM((FILTERS, ROWS, PAD, CHANNELS), BF16),
            ],
        ),
        out_shape=[
            jax.ShapeDtypeStruct((FILTERS, ROWS, PAD, CHANNELS), BF16),
            jax.ShapeDtypeStruct((2, CHANNELS, CHANNELS), BF16),
        ],
        compiler_params=pltpu.CompilerParams(vmem_limit_bytes=30 * MIB),
        name="stencil",
    )(place, tiles, own, lon_a, lon_b, lat_a, lat_b, cells)


SLAB = 32


def input_kernel(f, weight, *rest):
    out = rest[-1]
    total = 0.0
    for k in range(FILTERS):
        total += jnp.dot(f[k].reshape(ROWS * SLAB, CHANNELS), weight[k], preferred_element_type=F32)
    total = total.astype(BF16).reshape(ROWS, SLAB, CHANNELS)
    for b in range(SLAB // 16):
        out[b * 16 : (b + 1) * 16] = turned(total[:, b * 16 : (b + 1) * 16])


def input_gradient(f, weight, first, count, done=None):
    flops = 2 * ROWS * SLAB * count * FILTERS * CHANNELS * CHANNELS
    extra = [] if done is None else [done]
    return pl.pallas_call(
        input_kernel,
        grid=(count,),
        in_specs=[
            pl.BlockSpec((FILTERS, ROWS, SLAB, CHANNELS), lambda i: (0, 0, i + first, 0)),
            pl.BlockSpec((FILTERS, CHANNELS, CHANNELS), lambda i: (0, 0, 0)),
            *[pl.BlockSpec(memory_space=pl.ANY) for _ in extra],
        ],
        out_specs=pl.BlockSpec((SLAB, ROWS, CHANNELS), lambda i: (i + first, 0, 0)),
        out_shape=jax.ShapeDtypeStruct((COLS, ROWS, CHANNELS), BF16),
        input_output_aliases={2: 0} if extra else {},
        compiler_params=pltpu.CompilerParams(vmem_limit_bytes=20 * MIB),
        cost_estimate=pl.CostEstimate(flops=flops, bytes_accessed=4_000_000 * count, transcendentals=0),
        name="input_gradient",
    )(f, weight, *extra)


def own_half_kernel(place, f, cells, got, out):
    out[0] = (outer(f[0], cells[...]) + got[0].astype(F32)).astype(BF16)


def own_half(place, f, cells, got):
    block = (1, CHANNELS, CHANNELS)
    return pl.pallas_call(
        own_half_kernel,
        grid_spec=pltpu.PrefetchScalarGridSpec(
            num_scalar_prefetch=1,
            grid=(2,),
            in_specs=[
                pl.BlockSpec((1, ROWS, PAD, CHANNELS), lambda i, c: (2 * c[0] + i, 0, 0, 0)),
                pl.BlockSpec(cells.shape, lambda i, c: (0, 0, 0)),
                pl.BlockSpec(block, lambda i, c: (i, 0, 0)),
            ],
            out_specs=pl.BlockSpec(block, lambda i, c: (i, 0, 0)),
        ),
        out_shape=jax.ShapeDtypeStruct((2, CHANNELS, CHANNELS), BF16),
        compiler_params=pltpu.CompilerParams(vmem_limit_bytes=20 * MIB),
        name="own_half",
    )(place, f, cells, got)


def device(lat, lon):
    return lat * LON + lon % LON


def route(target):
    return [(device(a, b), device(*target(a, b))) for a in range(LAT) for b in range(LON)]


def lat_b_partner(a, b):
    if a in (0, LAT - 1):
        return a, b + LON // 2
    return (a + 1 if a % 2 else a - 1), b


LON_A = route(lambda a, b: (a, b ^ 1))
LON_B = route(lambda a, b: (a, b + 1 if b % 2 else b - 1))
LAT_A = route(lambda a, b: (a ^ 1, b))
LAT_B = route(lat_b_partner)
SIBLING = LAT_A


def along_z(mask):
    return route(lambda a, b: (a, b ^ mask))


def reversed_taps(basis, reach, band):
    span = basis.shape[2]
    offsets = jnp.arange(span, dtype=jnp.int32) - REACH
    masked = jnp.where(jnp.abs(offsets)[:, None] <= reach[None, :], basis, 0)
    total = masked.shape[3]
    slabs = []
    for q in range(TAPS):
        t = TAPS - 1 - q
        edge = jnp.zeros_like(masked[:, t, :, :1])
        first = masked[:, 0, :, :1] if q == 0 else edge
        last = masked[:, 2, :, total - 1 :] if q == 2 else edge
        padded = jnp.concatenate([first, masked[:, t], last], axis=2)
        slabs.append(lax.dynamic_slice_in_dim(padded, band * ROWS + q, ROWS, 2))
    taps = jnp.stack(slabs)[:, :, ::-1, :].astype(F32)
    taps = jnp.pad(jnp.transpose(taps, (3, 1, 0, 2)), ((0, 0), (0, 0), (0, 0), (0, SPAN - span)))
    taps = taps.reshape(ROWS, FILTERS, TAPS * SPAN)
    return jnp.pad(taps, ((0, 0), (0, 8 - FILTERS), (0, DEPTH - TAPS * SPAN)))


def edges_kernel(place, own, slab_a, slab_b, edge_a, edge_b, middle):
    even = place[1] == 0
    west, east = own[:REACH], own[COLS - REACH :]
    slab_a[...] = jnp.where(even, east, west)
    slab_b[...] = jnp.where(even, west, east)
    for slab, edge in ((slab_a, edge_a), (slab_b, edge_b)):
        block = turned(slab[...])
        edge[0], edge[1] = block[0], block[ROWS - 1]
    for b in range(PAD // 16):
        block = own[16 * b : min(16 * (b + 1), COLS)]
        if block.shape[0] < 16:
            block = jnp.concatenate([block, jnp.zeros((16 - block.shape[0], ROWS, CHANNELS), BF16)])
        block = turned(block)
        middle[0, 16 * b : 16 * (b + 1)] = block[0]
        middle[1, 16 * b : 16 * (b + 1)] = block[ROWS - 1]


def vmem_call(kernel, name, shapes, place, *args):
    whole = pl.BlockSpec(memory_space=pltpu.VMEM)
    return pl.pallas_call(
        kernel,
        in_specs=[pl.BlockSpec(memory_space=pltpu.SMEM)] + [whole] * len(args),
        out_specs=[whole] * len(shapes),
        out_shape=[jax.ShapeDtypeStruct(s, BF16) for s in shapes],
        compiler_params=pltpu.CompilerParams(vmem_limit_bytes=12 * MIB),
        name=name,
    )(place, *args)


def widen_kernel(place, middle, got_a, got_b, wide_a, wide_b):
    even, first = place[1] == 0, place[0] == 0
    left = jnp.where(even, got_b[...], got_a[...])
    right = jnp.where(even, got_a[...], got_b[...])
    for wide, is_last in ((wide_a, first), (wide_b, jnp.logical_not(first))):
        pick = lambda x: jnp.where(is_last, x[1], x[0])
        wide[COLS + REACH :] = jnp.zeros((WIDE - COLS - REACH, CHANNELS), BF16)
        wide[:REACH] = pick(left)
        wide[REACH : COLS + REACH] = pick(middle)[:COLS]
        wide[COLS + REACH : COLS + 2 * REACH] = pick(right)


def haloes(own, place):
    slab, edge, wide = (REACH, ROWS, CHANNELS), (2, REACH, CHANNELS), (WIDE, CHANNELS)
    slab_a, slab_b, edge_a, edge_b, middle = vmem_call(
        edges_kernel, "edges", [slab, slab, edge, edge, (2, PAD, CHANNELS)], place, own
    )
    edge_a = lax.ppermute(edge_a, AXES, LON_A)
    edge_b = lax.ppermute(edge_b, AXES, LON_B)
    lon_a = lax.ppermute(slab_a, AXES, LON_A)
    lon_b = lax.ppermute(slab_b, AXES, LON_B)
    wide_a, wide_b = vmem_call(widen_kernel, "widen", [wide, wide], place, middle, edge_a, edge_b)
    lat_a = lax.ppermute(wide_a, AXES, LAT_A)
    lat_b = lax.ppermute(wide_b, AXES, LAT_B)
    return lon_a, lon_b, lat_a, lat_b


def summed(parts, groups, axes):
    parts = lax.all_to_all(parts.reshape(groups, -1, CHANNELS), axes, 0, 0, tiled=True)
    return jnp.sum(parts.astype(F32), axis=0)


def on_device(cotangent, activations, weight, basis, reach):
    band = lax.axis_index(("y", "xh", "core"))
    core = lax.axis_index("core").astype(jnp.int32)
    odd = lax.axis_index("zl").astype(jnp.int32)
    place = jnp.stack([core, odd])
    own, act = jnp.swapaxes(cotangent, 0, 1), jnp.swapaxes(activations, 0, 1)
    around = haloes(own, place)
    tiles, cells = prepare(reversed_taps(basis, reach, band), act)
    f, send = stencil(place, tiles, own, *around, cells)
    got = lax.ppermute(send, AXES, SIBLING)
    grad_input = input_gradient(f, weight, 0, 2)
    got, grad_input = lax.optimization_barrier((got, grad_input))
    half = own_half(place, f, cells, got)
    part = lax.optimization_barrier(summed(half.reshape(-1, CHANNELS), 32, BLOCK).astype(BF16))
    others = [lax.ppermute(part, AXES, along_z(m)).astype(F32) for m in (2, 6, 4)]
    norm_factor = float(ROWS * COLS * LAT * LON) ** (-0.5)
    part = (part.astype(F32) + others[0]) + (others[1] + others[2])
    part = (part * norm_factor).astype(BF16)
    parts = lax.all_to_all(jnp.broadcast_to(part, (32, *part.shape)), BLOCK, 0, 0, tiled=True)
    mine = parts.reshape(2, CHANNELS, CHANNELS)
    theirs = lax.ppermute(mine, AXES, SIBLING)
    grad_weight = jnp.where(core == 0, jnp.concatenate([mine, theirs]), jnp.concatenate([theirs, mine]))
    grad_input = input_gradient(f, weight, 2, 1, grad_input)
    return jnp.swapaxes(grad_input, 0, 1), grad_weight


def solution(mesh):
    finer = Mesh(mesh.devices.reshape(4, 2, 2, 2, 4, 2), AXES)
    cells = P(("y", "xh", "core"), ("xl", "zh", "zl"), None)
    return jax.shard_map(
        on_device, mesh=finer, in_specs=(cells, cells, P(), P(), P()), out_specs=(cells, P()), check_vma=False
    )
```

```python
import functools

import jax
import jax.numpy as jnp
from jax import lax
from jax.experimental import pallas as pl
from jax.experimental.pallas import tpu as pltpu
from jax.sharding import Mesh, PartitionSpec as P

ROWS, COLS, REACH = 16, 90, 16
PAD, HALF, SPAN, WIDE = 96, 48, 80, 128
DEPTH = 256
CHANNELS, FILTERS, TAPS = 512, 4, 3
AXES = ("y", "xh", "core", "xl", "zh", "zl")
BLOCK = ("y", "xh", "xl", "zl")
LAT, LON = 16, 16
MIB = 1024 * 1024
BF16, F32 = jnp.bfloat16, jnp.float32


def turned(block):
    return jnp.swapaxes(block, 0, 1)


def local(kernel, name, shapes, inputs, scratch=(), spaces=None, aliases=None, mib=16, cost=None):
    spaces = spaces or {}
    spec = lambda i: pl.BlockSpec(memory_space=spaces.get(i, pltpu.VMEM))
    n = len(inputs)
    return pl.pallas_call(
        kernel,
        in_specs=[pl.BlockSpec(memory_space=pltpu.SMEM)] + [spec(i) for i in range(1, n)],
        out_specs=[spec(n + i) for i in range(len(shapes))],
        out_shape=[jax.ShapeDtypeStruct(shape, BF16) for shape in shapes],
        scratch_shapes=list(scratch),
        input_output_aliases=aliases or {},
        compiler_params=pltpu.CompilerParams(vmem_limit_bytes=mib * MIB),
        cost_estimate=cost and pl.CostEstimate(flops=cost, bytes_accessed=2_000_000, transcendentals=0),
        name=name,
    )(*inputs)


def edges_kernel(place, own, slab_a, slab_b, edge_a, edge_b, sides, sems):
    copies = [
        pltpu.make_async_copy(own.at[pl.ds(start, REACH)], sides.at[i], sems.at[i]) for i, start in enumerate((0, COLS - REACH))
    ]
    for copy in copies:
        copy.start()
    for copy in copies:
        copy.wait()
    even = place[1] == 0
    slab_a[...] = jnp.where(even, sides[1], sides[0])
    slab_b[...] = jnp.where(even, sides[0], sides[1])
    for slab, edge in ((slab_a, edge_a), (slab_b, edge_b)):
        block = turned(slab[...])
        edge[0], edge[1] = block[0], block[ROWS - 1]


def chunks():
    return [(b, 16 * b, min(16, COLS - 16 * b)) for b in range(PAD // 16)]


def fetches(source, target, sems):
    copies = [
        pltpu.make_async_copy(source.at[pl.ds(left, n)], target.at[pl.ds(left, n)], sems.at[b]) for b, left, n in chunks()
    ]
    for copy in copies:
        copy.start()
    return copies


def turned_chunk(block):
    if block.shape[0] < 16:
        block = jnp.concatenate([block, jnp.zeros((16 - block.shape[0], ROWS, CHANNELS), BF16)])
    return turned(block)


def turn_kernel(place, own, rows, middle, buffer, sems):
    copies = fetches(own, buffer, sems)
    for b, left, n in chunks():
        copies[b].wait()
        block = turned_chunk(buffer[left : left + n])
        rows[:, left : left + 16, :] = block
        middle[0, left : left + 16] = block[0]
        middle[1, left : left + 16] = block[ROWS - 1]


def widen_kernel(place, middle, got_a, got_b, wide_a, wide_b):
    even, first = place[1] == 0, place[0] == 0
    left = jnp.where(even, got_b[...], got_a[...])
    right = jnp.where(even, got_a[...], got_b[...])
    for wide, is_last in ((wide_a, first), (wide_b, jnp.logical_not(first))):
        pick = lambda x: jnp.where(is_last, x[1], x[0])
        wide[COLS + REACH :] = jnp.zeros((WIDE - COLS - REACH, CHANNELS), BF16)
        wide[:REACH] = pick(left)
        wide[REACH : COLS + REACH] = pick(middle)[:COLS]
        wide[COLS + REACH : COLS + 2 * REACH] = pick(right)


LEAD = 8


def prepare_kernel(place, basis, reach, act, tiles, cells, placed, buffer, sems):
    copies = fetches(act, buffer, sems)
    length = basis.shape[1]
    lats = basis.shape[2]
    offset = lax.broadcasted_iota(jnp.int32, (length, lats), 0) // FILTERS
    inside = jnp.abs(offset - REACH) <= reach[...]
    row = lax.broadcasted_iota(jnp.int32, (length, FILTERS * DEPTH), 0)
    col = lax.broadcasted_iota(jnp.int32, (length, FILTERS * DEPTH), 1)
    gap = jnp.where(row % FILTERS == col // DEPTH, col % DEPTH + row // FILTERS - 2 * REACH, -1)

    def put(t, q, lat):
        taps = jnp.where(inside, basis[t].astype(F32), 0.0)[:, lat].astype(BF16)
        ones = jnp.where(gap == SPAN * q, 1.0, 0.0).astype(BF16)
        return lax.dot_general(taps, ones, (((0,), (0,)), ((), ())), preferred_element_type=F32)

    for q in range(TAPS):
        placed[q, LEAD : LEAD + lats, :] = put(TAPS - 1 - q, q, slice(None))
    placed[0, LEAD - 1 : LEAD, :] = put(0, 0, slice(0, 128))[:1]
    placed[2, LEAD + lats : LEAD + lats + 1, :] = put(2, 2, slice(lats - 128, lats))[127:]
    start = place[2] * ROWS + LEAD - 1
    for r in range(ROWS):
        for k in range(FILTERS):
            lanes = pl.ds(k * DEPTH, DEPTH)
            taps = [placed[q, pl.ds(start + r + q, 1), lanes] for q in range(TAPS)]
            band = jnp.broadcast_to(taps[0] + taps[1] + taps[2], (HALF, DEPTH))
            tiles[r, k * HALF : (k + 1) * HALF, :] = pltpu.roll(band, 0, 1, stride=1, stride_axis=0).astype(BF16)
    for b, left, n in chunks():
        copies[b].wait()
        cells[:, left : left + 16, :] = turned_chunk(buffer[left : left + n])


GROUP = 4
STEPS = ROWS // GROUP


def outer(f, cells):
    f = f.reshape(ROWS * PAD, CHANNELS)
    cells = cells.reshape(ROWS * PAD, CHANNELS)
    return lax.dot_general(f, cells, (((0,), (0,)), ((), ())), preferred_element_type=F32)


def stencil_kernel(place, tiles, rows, lon_a, lon_b, lat_a, lat_b, cells_ref, f_out, send, low, high, held, cells, sem, f_sems):
    step = pl.program_id(0)
    stores = [
        pltpu.make_async_copy(held.at[:, pl.ds(GROUP * i, GROUP)], f_out.at[:, pl.ds(GROUP * i, GROUP)], f_sems.at[i])
        for i in range(STEPS)
    ]
    copy = pltpu.make_async_copy(cells_ref, cells, sem)

    @pl.when(step == 0)
    def _():
        copy.start()
        even, first = place[1] == 0, place[0] == 0
        inner = slice(1, ROWS + 1)
        low[inner, :REACH, :] = turned(jnp.where(even, lon_b[...], lon_a[...]))
        low[inner, REACH:, :] = rows[:, : SPAN - REACH, :]
        high[inner, : PAD - 32, :] = rows[:, 32:PAD, :]
        high[inner, PAD - 32 :, :] = jnp.zeros((ROWS, SPAN + 32 - PAD, CHANNELS), BF16)
        right = turned(jnp.where(even, lon_a[...], lon_b[...]))
        for r in range(ROWS):
            high[r + 1, COLS - 32 : COLS - 32 + REACH, :] = right[r]
        before = jnp.where(first, lat_b[...], lat_a[...])
        after = jnp.where(first, lat_a[...], lat_b[...])
        low[0], low[ROWS + 1] = before[:SPAN], after[:SPAN]
        high[0], high[ROWS + 1] = before[HALF:], after[HALF:]

    @pl.when(step < STEPS)
    def _():
        rest = jnp.zeros((DEPTH - TAPS * SPAN, CHANNELS), BF16)
        for j in range(GROUP):
            r = step * GROUP + j
            for h, source in enumerate((low, high)):
                taken = source[pl.ds(r, TAPS)].reshape(TAPS * SPAN, CHANNELS)
                taken = jnp.concatenate([taken, rest])
                f = jnp.dot(tiles[j], taken, preferred_element_type=F32).astype(BF16)
                f = f.reshape(FILTERS, HALF, CHANNELS)
                held[:, r, h * HALF : (h + 1) * HALF, :] = f

    for i, store in enumerate(stores):
        pl.when(step == i)(store.start)

    @pl.when(step == STEPS)
    def _():
        copy.wait()

    @pl.when(step >= STEPS)
    def _():
        k = 2 * (1 - place[0]) + step - STEPS
        send[0] = outer(held[k], cells[...]).astype(BF16)

    @pl.when(step == STEPS + 1)
    def _():
        for store in stores:
            store.wait()


def stencil(place, tiles, rows, lon_a, lon_b, lat_a, lat_b, cells):
    whole = lambda a: pl.BlockSpec(a.shape, lambda i, c: (0,) * a.ndim)
    return pl.pallas_call(
        stencil_kernel,
        grid_spec=pltpu.PrefetchScalarGridSpec(
            num_scalar_prefetch=1,
            grid=(STEPS + 2,),
            in_specs=[
                pl.BlockSpec((GROUP, FILTERS * HALF, DEPTH), lambda i, c: (jnp.minimum(i, STEPS - 1), 0, 0)),
                *[whole(a) for a in (rows, lon_a, lon_b, lat_a, lat_b)],
                pl.BlockSpec(memory_space=pl.ANY),
            ],
            out_specs=[
                pl.BlockSpec(memory_space=pltpu.HBM),
                pl.BlockSpec((1, CHANNELS, CHANNELS), lambda i, c: (jnp.maximum(i - STEPS, 0), 0, 0)),
            ],
            scratch_shapes=[
                pltpu.VMEM((ROWS + 2, SPAN, CHANNELS), BF16),
                pltpu.VMEM((ROWS + 2, SPAN, CHANNELS), BF16),
                pltpu.VMEM((FILTERS, ROWS, PAD, CHANNELS), BF16),
                pltpu.VMEM((ROWS, PAD, CHANNELS), BF16),
                pltpu.SemaphoreType.DMA(()),
                pltpu.SemaphoreType.DMA((STEPS,)),
            ],
        ),
        out_shape=[
            jax.ShapeDtypeStruct((FILTERS, ROWS, PAD, CHANNELS), BF16),
            jax.ShapeDtypeStruct((2, CHANNELS, CHANNELS), BF16),
        ],
        compiler_params=pltpu.CompilerParams(vmem_limit_bytes=30 * MIB),
        name="stencil",
    )(place, tiles, rows, lon_a, lon_b, lat_a, lat_b, cells)


SLAB = 32
SLABS = PAD // SLAB


def remainder_kernel(place, f_hbm, weight_hbm, cells_ref, out, mine, weight, f, cells, stage, weight_sems, f_sems, cells_sem, out_sems):
    loads = [pltpu.make_async_copy(weight_hbm.at[k], weight.at[k], weight_sems.at[k]) for k in range(FILTERS)]
    slabs = [
        [
            pltpu.make_async_copy(f_hbm.at[k, :, pl.ds(SLAB * j, SLAB)], f.at[k, :, pl.ds(SLAB * j, SLAB)], f_sems.at[j, k])
            for k in range(FILTERS)
        ]
        for j in range(SLABS)
    ]
    cells_copy = pltpu.make_async_copy(cells_ref, cells, cells_sem)
    for k in range(FILTERS):
        slabs[0][k].start()
        loads[k].start()
    for slab in slabs[1:]:
        for copy in slab:
            copy.start()
    cells_copy.start()
    stores = []
    for j in range(SLABS):
        left = SLAB * j
        cols = min(SLAB, COLS - left)
        total = 0.0
        for k in range(FILTERS):
            slabs[j][k].wait()
            if j == 0:
                loads[k].wait()
            taken = f[k, :, left : left + SLAB, :].reshape(ROWS * SLAB, CHANNELS)
            total += jnp.dot(taken, weight[k], preferred_element_type=F32)
        total = total.astype(BF16).reshape(ROWS, SLAB, CHANNELS)
        for b in range(SLAB // 16):
            stage[j, 16 * b : 16 * (b + 1)] = turned(total[:, 16 * b : 16 * (b + 1)])
        store = pltpu.make_async_copy(stage.at[j, pl.ds(0, cols)], out.at[pl.ds(left, cols)], out_sems.at[j])
        store.start()
        stores.append(store)
    cells_copy.wait()
    for j in range(2):
        mine[j] = outer(f[2 * place[0] + j], cells[...])
    for store in stores:
        store.wait()


def remainder(place, f, weight, cells):
    filtered = (FILTERS, ROWS, PAD, CHANNELS)
    half = (2, CHANNELS, CHANNELS)
    spec = lambda space: pl.BlockSpec(memory_space=space)
    flops = 2 * ROWS * PAD * (FILTERS + 2) * CHANNELS * CHANNELS
    return pl.pallas_call(
        remainder_kernel,
        in_specs=[spec(pltpu.SMEM), spec(pltpu.HBM), spec(pltpu.HBM), spec(pl.ANY)],
        out_specs=[spec(pl.ANY), spec(pltpu.VMEM)],
        out_shape=[jax.ShapeDtypeStruct((COLS, ROWS, CHANNELS), BF16), jax.ShapeDtypeStruct(half, F32)],
        scratch_shapes=[
            pltpu.VMEM((FILTERS, CHANNELS, CHANNELS), BF16),
            pltpu.VMEM(filtered, BF16),
            pltpu.VMEM((ROWS, PAD, CHANNELS), BF16),
            pltpu.VMEM((SLABS, SLAB, ROWS, CHANNELS), BF16),
            pltpu.SemaphoreType.DMA((FILTERS,)),
            pltpu.SemaphoreType.DMA((SLABS, FILTERS)),
            pltpu.SemaphoreType.DMA(()),
            pltpu.SemaphoreType.DMA((SLABS,)),
        ],
        compiler_params=pltpu.CompilerParams(vmem_limit_bytes=24 * MIB),
        cost_estimate=pl.CostEstimate(flops=flops, bytes_accessed=12_000_000, transcendentals=0),
        name="remainder",
    )(place, f, weight, cells)


def put_half_kernel(flip, place, half, *rest):
    out, sems = rest[-2:]
    start = 2 * (1 - place[0] if flip else place[0])
    part = CHANNELS // 4
    copies = [
        pltpu.make_async_copy(half.at[:, pl.ds(i * part, part)], out.at[pl.ds(start, 2), pl.ds(i * part, part)], sems.at[i])
        for i in range(4)
    ]
    for copy in copies:
        copy.start()
    for copy in copies:
        copy.wait()


def put_half(place, half, flip, done=()):
    inputs = [place, half, *done]
    spaces = {i: pl.ANY for i in range(1, len(inputs) + 1)}
    return local(
        functools.partial(put_half_kernel, flip), "put_half", [(FILTERS, CHANNELS, CHANNELS)], inputs,
        [pltpu.SemaphoreType.DMA((4,))], spaces, {2: 0} if done else {},
    )


def device(lat, lon):
    return lat * LON + lon % LON


def route(target):
    return [(device(a, b), device(*target(a, b))) for a in range(LAT) for b in range(LON)]


def lat_b_partner(a, b):
    if a in (0, LAT - 1):
        return a, b + LON // 2
    return (a + 1 if a % 2 else a - 1), b


LON_A = route(lambda a, b: (a, b ^ 1))
LON_B = route(lambda a, b: (a, b + 1 if b % 2 else b - 1))
LAT_A = route(lambda a, b: (a ^ 1, b))
LAT_B = route(lat_b_partner)
SIBLING = LAT_A


def along_z(mask):
    return route(lambda a, b: (a, b ^ mask))


def haloes(own, place):
    slab, edge, wide = (REACH, ROWS, CHANNELS), (2, REACH, CHANNELS), (WIDE, CHANNELS)
    slab_a, slab_b, edge_a, edge_b = local(
        edges_kernel, "edges", [slab, slab, edge, edge], [place, own],
        [pltpu.VMEM((2, *slab), BF16), pltpu.SemaphoreType.DMA((2,))], {1: pltpu.HBM},
    )
    own, edge_a, edge_b = lax.optimization_barrier((own, edge_a, edge_b))
    edge_a = lax.ppermute(edge_a, AXES, LON_A)
    edge_b = lax.ppermute(edge_b, AXES, LON_B)
    lon_a = lax.ppermute(slab_a, AXES, LON_A)
    lon_b = lax.ppermute(slab_b, AXES, LON_B)
    rows, middle = local(
        turn_kernel, "turn", [(ROWS, PAD, CHANNELS), (2, PAD, CHANNELS)], [place, own],
        [pltpu.VMEM(own.shape, BF16), pltpu.SemaphoreType.DMA((PAD // 16,))], {1: pltpu.HBM},
    )
    wide_a, wide_b = local(widen_kernel, "widen", [wide, wide], [place, middle, edge_a, edge_b])
    return rows, lon_a, lon_b, wide_a, wide_b


def prepared(place, basis, reach, act):
    taps, lats = basis.shape[2] * FILTERS, basis.shape[3]
    basis = jnp.transpose(basis, (1, 2, 0, 3)).reshape(TAPS, taps, lats)
    scratch = [
        pltpu.VMEM((TAPS, lats + 2 * LEAD, FILTERS * DEPTH), F32),
        pltpu.VMEM(act.shape, BF16),
        pltpu.SemaphoreType.DMA((PAD // 16,)),
    ]
    shapes = [(ROWS, FILTERS * HALF, DEPTH), (ROWS, PAD, CHANNELS)]
    inputs = [place, basis, reach.reshape(1, lats), act]
    return local(prepare_kernel, "prepare", shapes, inputs, scratch, {3: pltpu.HBM}, cost=100_000_000)


def summed(parts, groups, axes):
    parts = lax.all_to_all(parts.reshape(groups, -1, CHANNELS), axes, 0, 0, tiled=True)
    return jnp.sum(parts.astype(F32), axis=0)


def on_device(cotangent, activations, weight, basis, reach):
    band = lax.axis_index(("y", "xh", "core")).astype(jnp.int32)
    core = lax.axis_index("core").astype(jnp.int32)
    odd = lax.axis_index("zl").astype(jnp.int32)
    place = jnp.stack([core, odd, band])
    own, act = jnp.swapaxes(cotangent, 0, 1), jnp.swapaxes(activations, 0, 1)
    rows, lon_a, lon_b, wide_a, wide_b = haloes(own, place)
    act, wide_a, wide_b = lax.optimization_barrier((act, wide_a, wide_b))
    lat_a = lax.ppermute(wide_a, AXES, LAT_A)
    lat_b = lax.ppermute(wide_b, AXES, LAT_B)
    tiles, cells = prepared(place, basis, reach, act)
    f, send = stencil(place, tiles, rows, lon_a, lon_b, lat_a, lat_b, cells)
    got = lax.ppermute(send, AXES, SIBLING)
    grad_input, mine = remainder(place, f, weight, cells)
    got, mine = lax.optimization_barrier((got, mine))
    half = (mine + got.astype(F32)).astype(BF16)
    part = lax.optimization_barrier(summed(half.reshape(-1, CHANNELS), 32, BLOCK).astype(BF16))
    others = [lax.ppermute(part, AXES, along_z(m)).astype(F32) for m in (2, 6, 4)]
    norm_factor = float(ROWS * COLS * LAT * LON) ** (-0.5)
    part = (part.astype(F32) + others[0]) + (others[1] + others[2])
    part = (part * norm_factor).astype(BF16)
    parts = lax.all_to_all(jnp.broadcast_to(part, (32, *part.shape)), BLOCK, 0, 0, tiled=True)
    mine = parts.reshape(2, CHANNELS, CHANNELS)
    theirs = lax.ppermute(mine, AXES, SIBLING)
    grad_weight = put_half(place, mine, False)
    (grad_weight,) = put_half(place, theirs, True, grad_weight)
    return jnp.swapaxes(grad_input, 0, 1), grad_weight


def solution(mesh):
    finer = Mesh(mesh.devices.reshape(4, 2, 2, 2, 4, 2), AXES)
    cells = P(("y", "xh", "core"), ("xl", "zh", "zl"), None)
    return jax.shard_map(
        on_device, mesh=finer, in_specs=(cells, cells, P(), P(), P()), out_specs=(cells, P()), check_vma=False
    )
```

```python
import functools

import jax
import jax.numpy as jnp
from jax import lax
from jax.experimental import pallas as pl
from jax.experimental.pallas import tpu as pltpu
from jax.sharding import Mesh, PartitionSpec as P

ROWS, COLS, REACH = 16, 90, 16
PAD, HALF, SPAN, WIDE = 96, 48, 80, 128
DEPTH = 256
CHANNELS, FILTERS, TAPS = 512, 4, 3
AXES = ("y", "xh", "core", "xl", "zh", "zl")
BLOCK = ("y", "xh", "xl", "zl")
LAT, LON = 16, 16
MIB = 1024 * 1024
BF16, F32 = jnp.bfloat16, jnp.float32


def turned(block):
    return jnp.swapaxes(block, 0, 1)


def local(kernel, name, shapes, inputs, scratch=(), spaces=None, aliases=None, mib=16, cost=None):
    spaces = spaces or {}
    spec = lambda i: pl.BlockSpec(memory_space=spaces.get(i, pltpu.VMEM))
    n = len(inputs)
    return pl.pallas_call(
        kernel,
        in_specs=[pl.BlockSpec(memory_space=pltpu.SMEM)] + [spec(i) for i in range(1, n)],
        out_specs=[spec(n + i) for i in range(len(shapes))],
        out_shape=[jax.ShapeDtypeStruct(shape, BF16) for shape in shapes],
        scratch_shapes=list(scratch),
        input_output_aliases=aliases or {},
        compiler_params=pltpu.CompilerParams(vmem_limit_bytes=mib * MIB),
        cost_estimate=cost and pl.CostEstimate(flops=cost, bytes_accessed=2_000_000, transcendentals=0),
        name=name,
    )(*inputs)


def edges_kernel(place, own, slab_a, slab_b, edge_a, edge_b):
    even = place[1] == 0
    west, east = own[:REACH], own[COLS - REACH :]
    slab_a[...] = jnp.where(even, east, west)
    slab_b[...] = jnp.where(even, west, east)
    for slab, edge in ((slab_a, edge_a), (slab_b, edge_b)):
        block = turned(slab[...])
        edge[0], edge[1] = block[0], block[ROWS - 1]


def chunks():
    return [(b, 16 * b, min(16, COLS - 16 * b)) for b in range(PAD // 16)]


def fetches(source, target, sems):
    copies = [
        pltpu.make_async_copy(source.at[pl.ds(left, n)], target.at[pl.ds(left, n)], sems.at[b]) for b, left, n in chunks()
    ]
    for copy in copies:
        copy.start()
    return copies


def turned_chunk(block):
    if block.shape[0] < 16:
        block = jnp.concatenate([block, jnp.zeros((16 - block.shape[0], ROWS, CHANNELS), BF16)])
    return turned(block)


def turn_kernel(place, own, _, rows, middle, buffer, sems):
    copies = fetches(own, buffer, sems)
    for b, left, n in chunks():
        copies[b].wait()
        block = turned_chunk(buffer[left : left + n])
        rows[:, left : left + 16, :] = block
        middle[0, left : left + 16] = block[0]
        middle[1, left : left + 16] = block[ROWS - 1]


def widen_kernel(place, middle, got_a, got_b, wide_a, wide_b):
    even, first = place[1] == 0, place[0] == 0
    left = jnp.where(even, got_b[...], got_a[...])
    right = jnp.where(even, got_a[...], got_b[...])
    for wide, is_last in ((wide_a, first), (wide_b, jnp.logical_not(first))):
        pick = lambda x: jnp.where(is_last, x[1], x[0])
        wide[COLS + REACH :] = jnp.zeros((WIDE - COLS - REACH, CHANNELS), BF16)
        wide[:REACH] = pick(left)
        wide[REACH : COLS + REACH] = pick(middle)[:COLS]
        wide[COLS + REACH : COLS + 2 * REACH] = pick(right)


LEAD = 8


def prepare_kernel(place, basis, reach, act, _, tiles, cells, placed, buffer, sems):
    copies = fetches(act, buffer, sems)
    length = basis.shape[1]
    lats = basis.shape[2]
    offset = lax.broadcasted_iota(jnp.int32, (length, lats), 0) // FILTERS
    inside = jnp.abs(offset - REACH) <= reach[...]
    row = lax.broadcasted_iota(jnp.int32, (length, FILTERS * DEPTH), 0)
    col = lax.broadcasted_iota(jnp.int32, (length, FILTERS * DEPTH), 1)
    gap = jnp.where(row % FILTERS == col // DEPTH, col % DEPTH + row // FILTERS - 2 * REACH, -1)

    def put(t, q, lat):
        taps = jnp.where(inside, basis[t].astype(F32), 0.0)[:, lat].astype(BF16)
        ones = jnp.where(gap == SPAN * q, 1.0, 0.0).astype(BF16)
        return lax.dot_general(taps, ones, (((0,), (0,)), ((), ())), preferred_element_type=F32)

    for q in range(TAPS):
        placed[q, LEAD : LEAD + lats, :] = put(TAPS - 1 - q, q, slice(None))
    placed[0, LEAD - 1 : LEAD, :] = put(0, 0, slice(0, 128))[:1]
    placed[2, LEAD + lats : LEAD + lats + 1, :] = put(2, 2, slice(lats - 128, lats))[127:]
    start = place[2] * ROWS + LEAD - 1
    for r in range(ROWS):
        for k in range(FILTERS):
            lanes = pl.ds(k * DEPTH, DEPTH)
            taps = [placed[q, pl.ds(start + r + q, 1), lanes] for q in range(TAPS)]
            band = jnp.broadcast_to(taps[0] + taps[1] + taps[2], (HALF, DEPTH))
            tiles[r, k * HALF : (k + 1) * HALF, :] = pltpu.roll(band, 0, 1, stride=1, stride_axis=0).astype(BF16)
    for b, left, n in chunks():
        copies[b].wait()
        cells[:, left : left + 16, :] = turned_chunk(buffer[left : left + n])


GROUP = 4
STEPS = ROWS // GROUP


def outer(f, cells):
    f = f.reshape(ROWS * PAD, CHANNELS)
    cells = cells.reshape(ROWS * PAD, CHANNELS)
    return lax.dot_general(f, cells, (((0,), (0,)), ((), ())), preferred_element_type=F32)


def stencil_kernel(place, tiles, rows, lon_a, lon_b, lat_a, lat_b, cells_ref, f_out, send, low, high, held, cells, sem, f_sems):
    step = pl.program_id(0)
    stores = [
        pltpu.make_async_copy(held.at[:, pl.ds(GROUP * i, GROUP)], f_out.at[:, pl.ds(GROUP * i, GROUP)], f_sems.at[i])
        for i in range(STEPS)
    ]
    copy = pltpu.make_async_copy(cells_ref, cells, sem)

    @pl.when(step == 0)
    def _():
        copy.start()
        even, first = place[1] == 0, place[0] == 0
        inner = slice(1, ROWS + 1)
        low[inner, :REACH, :] = turned(jnp.where(even, lon_b[...], lon_a[...]))
        low[inner, REACH:, :] = rows[:, : SPAN - REACH, :]
        high[inner, : PAD - 32, :] = rows[:, 32:PAD, :]
        high[inner, PAD - 32 :, :] = jnp.zeros((ROWS, SPAN + 32 - PAD, CHANNELS), BF16)
        right = turned(jnp.where(even, lon_a[...], lon_b[...]))
        for r in range(ROWS):
            high[r + 1, COLS - 32 : COLS - 32 + REACH, :] = right[r]
        before = jnp.where(first, lat_b[...], lat_a[...])
        after = jnp.where(first, lat_a[...], lat_b[...])
        low[0], low[ROWS + 1] = before[:SPAN], after[:SPAN]
        high[0], high[ROWS + 1] = before[HALF:], after[HALF:]

    @pl.when(step < STEPS)
    def _():
        rest = jnp.zeros((DEPTH - TAPS * SPAN, CHANNELS), BF16)
        for j in range(GROUP):
            r = step * GROUP + j
            for h, source in enumerate((low, high)):
                taken = source[pl.ds(r, TAPS)].reshape(TAPS * SPAN, CHANNELS)
                taken = jnp.concatenate([taken, rest])
                f = jnp.dot(tiles[j], taken, preferred_element_type=F32).astype(BF16)
                f = f.reshape(FILTERS, HALF, CHANNELS)
                held[:, r, h * HALF : (h + 1) * HALF, :] = f

    for i, store in enumerate(stores):
        pl.when(step == i)(store.start)

    @pl.when(step == STEPS)
    def _():
        copy.wait()

    @pl.when(step >= STEPS)
    def _():
        k = 2 * (1 - place[0]) + step - STEPS
        send[0] = outer(held[k], cells[...]).astype(BF16)

    @pl.when(step == STEPS + 1)
    def _():
        for store in stores:
            store.wait()


def stencil(place, tiles, rows, lon_a, lon_b, lat_a, lat_b, cells):
    whole = lambda a: pl.BlockSpec(a.shape, lambda i, c: (0,) * a.ndim)
    return pl.pallas_call(
        stencil_kernel,
        grid_spec=pltpu.PrefetchScalarGridSpec(
            num_scalar_prefetch=1,
            grid=(STEPS + 2,),
            in_specs=[
                pl.BlockSpec((GROUP, FILTERS * HALF, DEPTH), lambda i, c: (jnp.minimum(i, STEPS - 1), 0, 0)),
                *[whole(a) for a in (rows, lon_a, lon_b, lat_a, lat_b)],
                pl.BlockSpec(memory_space=pl.ANY),
            ],
            out_specs=[
                pl.BlockSpec(memory_space=pltpu.HBM),
                pl.BlockSpec((1, CHANNELS, CHANNELS), lambda i, c: (jnp.maximum(i - STEPS, 0), 0, 0)),
            ],
            scratch_shapes=[
                pltpu.VMEM((ROWS + 2, SPAN, CHANNELS), BF16),
                pltpu.VMEM((ROWS + 2, SPAN, CHANNELS), BF16),
                pltpu.VMEM((FILTERS, ROWS, PAD, CHANNELS), BF16),
                pltpu.VMEM((ROWS, PAD, CHANNELS), BF16),
                pltpu.SemaphoreType.DMA(()),
                pltpu.SemaphoreType.DMA((STEPS,)),
            ],
        ),
        out_shape=[
            jax.ShapeDtypeStruct((FILTERS, ROWS, PAD, CHANNELS), BF16),
            jax.ShapeDtypeStruct((2, CHANNELS, CHANNELS), BF16),
        ],
        compiler_params=pltpu.CompilerParams(vmem_limit_bytes=30 * MIB),
        name="stencil",
    )(place, tiles, rows, lon_a, lon_b, lat_a, lat_b, cells)


SLAB = 32
SLABS = PAD // SLAB


def remainder_kernel(place, f_hbm, weight_hbm, cells_ref, out, mine, weight, f, cells, stage, weight_sems, f_sems, cells_sem, out_sems):
    loads = [pltpu.make_async_copy(weight_hbm.at[k], weight.at[k], weight_sems.at[k]) for k in range(FILTERS)]
    slabs = [
        [
            pltpu.make_async_copy(f_hbm.at[k, :, pl.ds(SLAB * j, SLAB)], f.at[k, :, pl.ds(SLAB * j, SLAB)], f_sems.at[j, k])
            for k in range(FILTERS)
        ]
        for j in range(SLABS)
    ]
    cells_copy = pltpu.make_async_copy(cells_ref, cells, cells_sem)
    for k in range(FILTERS):
        slabs[0][k].start()
        loads[k].start()
    for slab in slabs[1:]:
        for copy in slab:
            copy.start()
    cells_copy.start()
    stores = []
    for j in range(SLABS):
        left = SLAB * j
        cols = min(SLAB, COLS - left)
        total = 0.0
        for k in range(FILTERS):
            slabs[j][k].wait()
            if j == 0:
                loads[k].wait()
            taken = f[k, :, left : left + SLAB, :].reshape(ROWS * SLAB, CHANNELS)
            total += jnp.dot(taken, weight[k], preferred_element_type=F32)
        total = total.astype(BF16).reshape(ROWS, SLAB, CHANNELS)
        for b in range(SLAB // 16):
            stage[j, 16 * b : 16 * (b + 1)] = turned(total[:, 16 * b : 16 * (b + 1)])
        store = pltpu.make_async_copy(stage.at[j, pl.ds(0, cols)], out.at[pl.ds(left, cols)], out_sems.at[j])
        store.start()
        stores.append(store)
    cells_copy.wait()
    for j in range(2):
        mine[j] = outer(f[2 * place[0] + j], cells[...])
    for store in stores:
        store.wait()


def remainder(place, f, weight, cells):
    filtered = (FILTERS, ROWS, PAD, CHANNELS)
    half = (2, CHANNELS, CHANNELS)
    spec = lambda space: pl.BlockSpec(memory_space=space)
    flops = 2 * ROWS * PAD * (FILTERS + 2) * CHANNELS * CHANNELS
    return pl.pallas_call(
        remainder_kernel,
        in_specs=[spec(pltpu.SMEM), spec(pltpu.HBM), spec(pltpu.HBM), spec(pl.ANY)],
        out_specs=[spec(pl.ANY), spec(pltpu.VMEM)],
        out_shape=[jax.ShapeDtypeStruct((COLS, ROWS, CHANNELS), BF16), jax.ShapeDtypeStruct(half, F32)],
        scratch_shapes=[
            pltpu.VMEM((FILTERS, CHANNELS, CHANNELS), BF16),
            pltpu.VMEM(filtered, BF16),
            pltpu.VMEM((ROWS, PAD, CHANNELS), BF16),
            pltpu.VMEM((SLABS, SLAB, ROWS, CHANNELS), BF16),
            pltpu.SemaphoreType.DMA((FILTERS,)),
            pltpu.SemaphoreType.DMA((SLABS, FILTERS)),
            pltpu.SemaphoreType.DMA(()),
            pltpu.SemaphoreType.DMA((SLABS,)),
        ],
        compiler_params=pltpu.CompilerParams(vmem_limit_bytes=24 * MIB),
        cost_estimate=pl.CostEstimate(flops=flops, bytes_accessed=12_000_000, transcendentals=0),
        name="remainder",
    )(place, f, weight, cells)


def put_half_kernel(flip, place, half, *rest):
    out, sems = rest[-2:]
    start = 2 * (1 - place[0] if flip else place[0])
    part = CHANNELS // 4
    copies = [
        pltpu.make_async_copy(half.at[:, pl.ds(i * part, part)], out.at[pl.ds(start, 2), pl.ds(i * part, part)], sems.at[i])
        for i in range(4)
    ]
    for copy in copies:
        copy.start()
    for copy in copies:
        copy.wait()


def put_half(place, half, flip, done=()):
    inputs = [place, half, *done]
    spaces = {i: pl.ANY for i in range(1, len(inputs) + 1)}
    return local(
        functools.partial(put_half_kernel, flip), "put_half", [(FILTERS, CHANNELS, CHANNELS)], inputs,
        [pltpu.SemaphoreType.DMA((4,))], spaces, {2: 0} if done else {},
    )


def device(lat, lon):
    return lat * LON + lon % LON


def route(target):
    return [(device(a, b), device(*target(a, b))) for a in range(LAT) for b in range(LON)]


def lat_b_partner(a, b):
    if a in (0, LAT - 1):
        return a, b + LON // 2
    return (a + 1 if a % 2 else a - 1), b


LON_A = route(lambda a, b: (a, b ^ 1))
LON_B = route(lambda a, b: (a, b + 1 if b % 2 else b - 1))
LAT_A = route(lambda a, b: (a ^ 1, b))
LAT_B = route(lat_b_partner)
SIBLING = LAT_A


def along_z(mask):
    return route(lambda a, b: (a, b ^ mask))


def haloes(own, place):
    slab, edge, wide = (REACH, ROWS, CHANNELS), (2, REACH, CHANNELS), (WIDE, CHANNELS)
    slab_a, slab_b, edge_a, edge_b = local(edges_kernel, "edges", [slab, slab, edge, edge], [place, own])
    rows, middle = local(
        turn_kernel, "turn", [(ROWS, PAD, CHANNELS), (2, PAD, CHANNELS)], [place, own, edge_a],
        [pltpu.VMEM(own.shape, BF16), pltpu.SemaphoreType.DMA((PAD // 16,))], {1: pltpu.HBM, 2: pl.ANY}, cost=4_000_000_000,
    )
    edge_a = lax.ppermute(edge_a, AXES, LON_A)
    edge_b = lax.ppermute(edge_b, AXES, LON_B)
    lon_a = lax.ppermute(slab_a, AXES, LON_A)
    lon_b = lax.ppermute(slab_b, AXES, LON_B)
    wide_a, wide_b = local(widen_kernel, "widen", [wide, wide], [place, middle, edge_a, edge_b])
    return rows, lon_a, lon_b, wide_a, wide_b


def prepared(place, basis, reach, act, after):
    taps, lats = basis.shape[2] * FILTERS, basis.shape[3]
    basis = jnp.transpose(basis, (1, 2, 0, 3)).reshape(TAPS, taps, lats)
    scratch = [
        pltpu.VMEM((TAPS, lats + 2 * LEAD, FILTERS * DEPTH), F32),
        pltpu.VMEM(act.shape, BF16),
        pltpu.SemaphoreType.DMA((PAD // 16,)),
    ]
    shapes = [(ROWS, FILTERS * HALF, DEPTH), (ROWS, PAD, CHANNELS)]
    inputs = [place, basis, reach.reshape(1, lats), act, after]
    return local(prepare_kernel, "prepare", shapes, inputs, scratch, {3: pltpu.HBM, 4: pl.ANY}, cost=1_000_000_000)


def summed(parts, groups, axes):
    parts = lax.all_to_all(parts.reshape(groups, -1, CHANNELS), axes, 0, 0, tiled=True)
    return jnp.sum(parts.astype(F32), axis=0)


def on_device(cotangent, activations, weight, basis, reach):
    band = lax.axis_index(("y", "xh", "core")).astype(jnp.int32)
    core = lax.axis_index("core").astype(jnp.int32)
    odd = lax.axis_index("zl").astype(jnp.int32)
    place = jnp.stack([core, odd, band])
    own, act = jnp.swapaxes(cotangent, 0, 1), jnp.swapaxes(activations, 0, 1)
    rows, lon_a, lon_b, wide_a, wide_b = haloes(own, place)
    lat_a = lax.ppermute(wide_a, AXES, LAT_A)
    lat_b = lax.ppermute(wide_b, AXES, LAT_B)
    tiles, cells = prepared(place, basis, reach, act, wide_a)
    f, send = stencil(place, tiles, rows, lon_a, lon_b, lat_a, lat_b, cells)
    got = lax.ppermute(send, AXES, SIBLING)
    grad_input, mine = remainder(place, f, weight, cells)
    half = (mine + got.astype(F32)).astype(BF16)
    part = lax.optimization_barrier(summed(half.reshape(-1, CHANNELS), 32, BLOCK).astype(BF16))
    others = [lax.ppermute(part, AXES, along_z(m)).astype(F32) for m in (2, 6, 4)]
    norm_factor = float(ROWS * COLS * LAT * LON) ** (-0.5)
    part = (part.astype(F32) + others[0]) + (others[1] + others[2])
    part = (part * norm_factor).astype(BF16)
    parts = lax.all_to_all(jnp.broadcast_to(part, (32, *part.shape)), BLOCK, 0, 0, tiled=True)
    mine = parts.reshape(2, CHANNELS, CHANNELS)
    theirs = lax.ppermute(mine, AXES, SIBLING)
    grad_weight = put_half(place, mine, False)
    (grad_weight,) = put_half(place, theirs, True, grad_weight)
    return jnp.swapaxes(grad_input, 0, 1), grad_weight


def solution(mesh):
    finer = Mesh(mesh.devices.reshape(4, 2, 2, 2, 4, 2), AXES)
    cells = P(("y", "xh", "core"), ("xl", "zh", "zl"), None)
    return jax.shard_map(
        on_device, mesh=finer, in_specs=(cells, cells, P(), P(), P()), out_specs=(cells, P()), check_vma=False
    )
```

```python
import functools

import jax
import jax.numpy as jnp
from jax import lax
from jax.experimental import pallas as pl
from jax.experimental.pallas import tpu as pltpu
from jax.sharding import Mesh, PartitionSpec as P

ROWS, COLS, REACH = 16, 90, 16
PAD, HALF, SPAN, WIDE = 96, 48, 80, 128
DEPTH = 256
CHANNELS, FILTERS, TAPS = 512, 4, 3
AXES = ("y", "xh", "core", "xl", "zh", "zl")
BLOCK = ("y", "xh", "xl", "zl")
LAT, LON = 16, 16
MIB = 1024 * 1024
BF16, F32 = jnp.bfloat16, jnp.float32


def turned(block):
    return jnp.swapaxes(block, 0, 1)


def local(kernel, name, shapes, inputs, scratch=(), spaces=None, aliases=None, mib=16, cost=None):
    spaces = spaces or {}
    spec = lambda i: pl.BlockSpec(memory_space=spaces.get(i, pltpu.VMEM))
    n = len(inputs)
    return pl.pallas_call(
        kernel,
        in_specs=[pl.BlockSpec(memory_space=pltpu.SMEM)] + [spec(i) for i in range(1, n)],
        out_specs=[spec(n + i) for i in range(len(shapes))],
        out_shape=[jax.ShapeDtypeStruct(shape, BF16) for shape in shapes],
        scratch_shapes=list(scratch),
        input_output_aliases=aliases or {},
        compiler_params=pltpu.CompilerParams(vmem_limit_bytes=mib * MIB),
        cost_estimate=cost and pl.CostEstimate(flops=cost, bytes_accessed=2_000_000, transcendentals=0),
        name=name,
    )(*inputs)


def edges_kernel(place, own, slab_a, slab_b, edge_a, edge_b):
    even = place[1] == 0
    west, east = own[:REACH], own[COLS - REACH :]
    slab_a[...] = jnp.where(even, east, west)
    slab_b[...] = jnp.where(even, west, east)
    for slab, edge in ((slab_a, edge_a), (slab_b, edge_b)):
        block = turned(slab[...])
        edge[0], edge[1] = block[0], block[ROWS - 1]


def chunks():
    return [(b, 16 * b, min(16, COLS - 16 * b)) for b in range(PAD // 16)]


def fetches(source, target, sems):
    copies = [
        pltpu.make_async_copy(source.at[pl.ds(left, n)], target.at[pl.ds(left, n)], sems.at[b]) for b, left, n in chunks()
    ]
    for copy in copies:
        copy.start()
    return copies


def turned_chunk(block):
    if block.shape[0] < 16:
        block = jnp.concatenate([block, jnp.zeros((16 - block.shape[0], ROWS, CHANNELS), BF16)])
    return turned(block)


def turn_kernel(place, own, _, rows, middle, buffer, sems):
    copies = fetches(own, buffer, sems)
    for b, left, n in chunks():
        copies[b].wait()
        block = turned_chunk(buffer[left : left + n])
        rows[:, left : left + 16, :] = block
        middle[0, left : left + 16] = block[0]
        middle[1, left : left + 16] = block[ROWS - 1]


def widen_kernel(place, middle, got_a, got_b, wide_a, wide_b):
    even, first = place[1] == 0, place[0] == 0
    left = jnp.where(even, got_b[...], got_a[...])
    right = jnp.where(even, got_a[...], got_b[...])
    for wide, is_last in ((wide_a, first), (wide_b, jnp.logical_not(first))):
        pick = lambda x: jnp.where(is_last, x[1], x[0])
        wide[COLS + REACH :] = jnp.zeros((WIDE - COLS - REACH, CHANNELS), BF16)
        wide[:REACH] = pick(left)
        wide[REACH : COLS + REACH] = pick(middle)[:COLS]
        wide[COLS + REACH : COLS + 2 * REACH] = pick(right)


LEAD = 8


def prepare_kernel(place, basis, reach, act, _, tiles, cells, placed, buffer, sems):
    copies = fetches(act, buffer, sems)
    length = basis.shape[1] * FILTERS
    lats = basis.shape[3]
    offset = lax.broadcasted_iota(jnp.int32, (length, lats), 0) // FILTERS
    inside = jnp.abs(offset - REACH) <= reach[...]
    row = lax.broadcasted_iota(jnp.int32, (length, FILTERS * DEPTH), 0)
    col = lax.broadcasted_iota(jnp.int32, (length, FILTERS * DEPTH), 1)
    gap = jnp.where(row % FILTERS == col // DEPTH, col % DEPTH + row // FILTERS - 2 * REACH, -1)

    def put(t, q, lat):
        taps = jnp.where(inside, basis[t].astype(F32).reshape(length, lats), 0.0)[:, lat].astype(BF16)
        ones = jnp.where(gap == SPAN * q, 1.0, 0.0).astype(BF16)
        return lax.dot_general(taps, ones, (((0,), (0,)), ((), ())), preferred_element_type=F32)

    for q in range(TAPS):
        placed[q, LEAD : LEAD + lats, :] = put(TAPS - 1 - q, q, slice(None))
    placed[0, LEAD - 1 : LEAD, :] = put(0, 0, slice(0, 128))[:1]
    placed[2, LEAD + lats : LEAD + lats + 1, :] = put(2, 2, slice(lats - 128, lats))[127:]
    start = place[2] * ROWS + LEAD - 1
    for r in range(ROWS):
        for k in range(FILTERS):
            lanes = pl.ds(k * DEPTH, DEPTH)
            taps = [placed[q, pl.ds(start + r + q, 1), lanes] for q in range(TAPS)]
            band = jnp.broadcast_to(taps[0] + taps[1] + taps[2], (HALF, DEPTH))
            tiles[r, k * HALF : (k + 1) * HALF, :] = pltpu.roll(band, 0, 1, stride=1, stride_axis=0).astype(BF16)
    for b, left, n in chunks():
        copies[b].wait()
        cells[:, left : left + 16, :] = turned_chunk(buffer[left : left + n])


GROUP = 4
STEPS = ROWS // GROUP


def outer(f, cells):
    f = f.reshape(ROWS * PAD, CHANNELS)
    cells = cells.reshape(ROWS * PAD, CHANNELS)
    return lax.dot_general(f, cells, (((0,), (0,)), ((), ())), preferred_element_type=F32)


def stencil_kernel(place, tiles, rows, lon_a, lon_b, lat_a, lat_b, cells_ref, f_out, send, low, high, held, cells, sem, f_sems):
    step = pl.program_id(0)
    stores = [
        pltpu.make_async_copy(held.at[:, pl.ds(GROUP * i, GROUP)], f_out.at[:, pl.ds(GROUP * i, GROUP)], f_sems.at[i])
        for i in range(STEPS)
    ]
    copy = pltpu.make_async_copy(cells_ref, cells, sem)

    @pl.when(step == 0)
    def _():
        copy.start()
        even, first = place[1] == 0, place[0] == 0
        inner = slice(1, ROWS + 1)
        low[inner, :REACH, :] = turned(jnp.where(even, lon_b[...], lon_a[...]))
        low[inner, REACH:, :] = rows[:, : SPAN - REACH, :]
        high[inner, : PAD - 32, :] = rows[:, 32:PAD, :]
        high[inner, PAD - 32 :, :] = jnp.zeros((ROWS, SPAN + 32 - PAD, CHANNELS), BF16)
        right = turned(jnp.where(even, lon_a[...], lon_b[...]))
        for r in range(ROWS):
            high[r + 1, COLS - 32 : COLS - 32 + REACH, :] = right[r]
        before = jnp.where(first, lat_b[...], lat_a[...])
        after = jnp.where(first, lat_a[...], lat_b[...])
        low[0], low[ROWS + 1] = before[:SPAN], after[:SPAN]
        high[0], high[ROWS + 1] = before[HALF:], after[HALF:]

    @pl.when(step < STEPS)
    def _():
        rest = jnp.zeros((DEPTH - TAPS * SPAN, CHANNELS), BF16)
        for j in range(GROUP):
            r = step * GROUP + j
            for h, source in enumerate((low, high)):
                taken = source[pl.ds(r, TAPS)].reshape(TAPS * SPAN, CHANNELS)
                taken = jnp.concatenate([taken, rest])
                f = jnp.dot(tiles[j], taken, preferred_element_type=F32).astype(BF16)
                f = f.reshape(FILTERS, HALF, CHANNELS)
                held[:, r, h * HALF : (h + 1) * HALF, :] = f

    for i, store in enumerate(stores):
        pl.when(step == i)(store.start)

    @pl.when(step == STEPS)
    def _():
        copy.wait()

    @pl.when(step >= STEPS)
    def _():
        k = 2 * (1 - place[0]) + step - STEPS
        send[0] = outer(held[k], cells[...]).astype(BF16)

    @pl.when(step == STEPS + 1)
    def _():
        for store in stores:
            store.wait()


def stencil(place, tiles, rows, lon_a, lon_b, lat_a, lat_b, cells):
    whole = lambda a: pl.BlockSpec(a.shape, lambda i, c: (0,) * a.ndim)
    return pl.pallas_call(
        stencil_kernel,
        grid_spec=pltpu.PrefetchScalarGridSpec(
            num_scalar_prefetch=1,
            grid=(STEPS + 2,),
            in_specs=[
                pl.BlockSpec((GROUP, FILTERS * HALF, DEPTH), lambda i, c: (jnp.minimum(i, STEPS - 1), 0, 0)),
                *[whole(a) for a in (rows, lon_a, lon_b, lat_a, lat_b)],
                pl.BlockSpec(memory_space=pl.ANY),
            ],
            out_specs=[
                pl.BlockSpec(memory_space=pltpu.HBM),
                pl.BlockSpec((1, CHANNELS, CHANNELS), lambda i, c: (jnp.maximum(i - STEPS, 0), 0, 0)),
            ],
            scratch_shapes=[
                pltpu.VMEM((ROWS + 2, SPAN, CHANNELS), BF16),
                pltpu.VMEM((ROWS + 2, SPAN, CHANNELS), BF16),
                pltpu.VMEM((FILTERS, ROWS, PAD, CHANNELS), BF16),
                pltpu.VMEM((ROWS, PAD, CHANNELS), BF16),
                pltpu.SemaphoreType.DMA(()),
                pltpu.SemaphoreType.DMA((STEPS,)),
            ],
        ),
        out_shape=[
            jax.ShapeDtypeStruct((FILTERS, ROWS, PAD, CHANNELS), BF16),
            jax.ShapeDtypeStruct((2, CHANNELS, CHANNELS), BF16),
        ],
        compiler_params=pltpu.CompilerParams(vmem_limit_bytes=30 * MIB),
        name="stencil",
    )(place, tiles, rows, lon_a, lon_b, lat_a, lat_b, cells)


def own_part_kernel(place, f_hbm, cells_ref, mine, f, cells, sems):
    copies = [pltpu.make_async_copy(f_hbm.at[2 * place[0] + j], f.at[j], sems.at[j]) for j in range(2)]
    copies.append(pltpu.make_async_copy(cells_ref, cells, sems.at[2]))
    for copy in (copies[2], copies[0], copies[1]):
        copy.start()
    copies[2].wait()
    for j in range(2):
        copies[j].wait()
        mine[j] = outer(f[j], cells[...])


def spec(space):
    return pl.BlockSpec(memory_space=space)


def own_part(place, f, cells):
    return pl.pallas_call(
        own_part_kernel,
        in_specs=[spec(pltpu.SMEM), spec(pl.ANY), spec(pl.ANY)],
        out_specs=spec(pltpu.VMEM),
        out_shape=jax.ShapeDtypeStruct((2, CHANNELS, CHANNELS), F32),
        scratch_shapes=[
            pltpu.VMEM((2, ROWS, PAD, CHANNELS), BF16),
            pltpu.VMEM((ROWS, PAD, CHANNELS), BF16),
            pltpu.SemaphoreType.DMA((3,)),
        ],
        compiler_params=pltpu.CompilerParams(vmem_limit_bytes=16 * MIB),
        cost_estimate=pl.CostEstimate(flops=4 * ROWS * PAD * CHANNELS**2, bytes_accessed=6_000_000, transcendentals=0),
        name="own_part",
    )(place, f, cells)


SLAB = 32
SLABS = PAD // SLAB


def input_kernel(f_hbm, weight_hbm, out, weight, f, stage, weight_sems, f_sems, out_sems):
    loads = [pltpu.make_async_copy(weight_hbm.at[k], weight.at[k], weight_sems.at[k]) for k in range(FILTERS)]
    slabs = []
    for j in range(SLABS):
        at = pl.ds(SLAB * j, SLAB)
        slabs.append([pltpu.make_async_copy(f_hbm.at[k, :, at], f.at[k, :, at], f_sems.at[j, k]) for k in range(FILTERS)])
    for k in range(FILTERS):
        slabs[0][k].start()
        loads[k].start()
    for slab in slabs[1:]:
        for copy in slab:
            copy.start()
    stores = []
    for j in range(SLABS):
        left = SLAB * j
        cols = min(SLAB, COLS - left)
        total = 0.0
        for k in range(FILTERS):
            slabs[j][k].wait()
            if j == 0:
                loads[k].wait()
            taken = f[k, :, left : left + SLAB, :].reshape(ROWS * SLAB, CHANNELS)
            total += jnp.dot(taken, weight[k], preferred_element_type=F32)
        total = total.astype(BF16).reshape(ROWS, SLAB, CHANNELS)
        for b in range(SLAB // 16):
            stage[j, 16 * b : 16 * (b + 1)] = turned(total[:, 16 * b : 16 * (b + 1)])
        store = pltpu.make_async_copy(stage.at[j, pl.ds(0, cols)], out.at[pl.ds(left, cols)], out_sems.at[j])
        store.start()
        stores.append(store)
    for store in stores:
        store.wait()


def input_gradient(f, weight):
    flops = 2 * ROWS * PAD * FILTERS * CHANNELS * CHANNELS
    return pl.pallas_call(
        input_kernel,
        in_specs=[spec(pl.ANY), spec(pltpu.HBM)],
        out_specs=spec(pl.ANY),
        out_shape=jax.ShapeDtypeStruct((COLS, ROWS, CHANNELS), BF16),
        scratch_shapes=[
            pltpu.VMEM((FILTERS, CHANNELS, CHANNELS), BF16),
            pltpu.VMEM((FILTERS, ROWS, PAD, CHANNELS), BF16),
            pltpu.VMEM((SLABS, SLAB, ROWS, CHANNELS), BF16),
            pltpu.SemaphoreType.DMA((FILTERS,)),
            pltpu.SemaphoreType.DMA((SLABS, FILTERS)),
            pltpu.SemaphoreType.DMA((SLABS,)),
        ],
        compiler_params=pltpu.CompilerParams(vmem_limit_bytes=20 * MIB),
        cost_estimate=pl.CostEstimate(flops=flops, bytes_accessed=10_000_000, transcendentals=0),
        name="input_gradient",
    )(f, weight)


def put_half_kernel(flip, place, half, *rest):
    out, sems = rest[-2:]
    start = 2 * (1 - place[0] if flip else place[0])
    part = CHANNELS // 4
    copies = [
        pltpu.make_async_copy(half.at[:, pl.ds(i * part, part)], out.at[pl.ds(start, 2), pl.ds(i * part, part)], sems.at[i])
        for i in range(4)
    ]
    for copy in copies:
        copy.start()
    for copy in copies:
        copy.wait()


def put_half(place, half, flip, done=()):
    inputs = [place, half, *done]
    spaces = {i: pl.ANY for i in range(1, len(inputs) + 1)}
    return local(
        functools.partial(put_half_kernel, flip), "put_half", [(FILTERS, CHANNELS, CHANNELS)], inputs,
        [pltpu.SemaphoreType.DMA((4,))], spaces, {2: 0} if done else {},
    )


def device(lat, lon):
    return lat * LON + lon % LON


def route(target):
    return [(device(a, b), device(*target(a, b))) for a in range(LAT) for b in range(LON)]


def lat_b_partner(a, b):
    if a in (0, LAT - 1):
        return a, b + LON // 2
    return (a + 1 if a % 2 else a - 1), b


LON_A = route(lambda a, b: (a, b ^ 1))
LON_B = route(lambda a, b: (a, b + 1 if b % 2 else b - 1))
LAT_A = route(lambda a, b: (a ^ 1, b))
LAT_B = route(lat_b_partner)
SIBLING = LAT_A


def along_z(mask):
    return route(lambda a, b: (a, b ^ mask))


def haloes(own, place):
    slab, edge, wide = (REACH, ROWS, CHANNELS), (2, REACH, CHANNELS), (WIDE, CHANNELS)
    slab_a, slab_b, edge_a, edge_b = local(edges_kernel, "edges", [slab, slab, edge, edge], [place, own])
    rows, middle = local(
        turn_kernel, "turn", [(ROWS, PAD, CHANNELS), (2, PAD, CHANNELS)], [place, own, edge_a],
        [pltpu.VMEM(own.shape, BF16), pltpu.SemaphoreType.DMA((PAD // 16,))], {1: pltpu.HBM, 2: pl.ANY}, cost=4_000_000_000,
    )
    edge_a = lax.ppermute(edge_a, AXES, LON_A)
    edge_b = lax.ppermute(edge_b, AXES, LON_B)
    lon_a = lax.ppermute(slab_a, AXES, LON_A)
    lon_b = lax.ppermute(slab_b, AXES, LON_B)
    wide_a, wide_b = local(widen_kernel, "widen", [wide, wide], [place, middle, edge_a, edge_b])
    return rows, lon_a, lon_b, wide_a, wide_b


def prepared(place, basis, reach, act, after):
    lats = basis.shape[3]
    basis = jnp.transpose(basis, (1, 2, 0, 3))
    scratch = [
        pltpu.VMEM((TAPS, lats + 2 * LEAD, FILTERS * DEPTH), F32),
        pltpu.VMEM(act.shape, BF16),
        pltpu.SemaphoreType.DMA((PAD // 16,)),
    ]
    shapes = [(ROWS, FILTERS * HALF, DEPTH), (ROWS, PAD, CHANNELS)]
    inputs = [place, basis, reach.reshape(1, lats), act, after]
    return local(prepare_kernel, "prepare", shapes, inputs, scratch, {3: pltpu.HBM, 4: pl.ANY}, cost=1_000_000_000)


def summed(parts, groups, axes):
    parts = lax.all_to_all(parts.reshape(groups, -1, CHANNELS), axes, 0, 0, tiled=True)
    return jnp.sum(parts.astype(F32), axis=0)


def on_device(cotangent, activations, weight, basis, reach):
    band = lax.axis_index(("y", "xh", "core")).astype(jnp.int32)
    core = lax.axis_index("core").astype(jnp.int32)
    odd = lax.axis_index("zl").astype(jnp.int32)
    place = jnp.stack([core, odd, band])
    own, act = jnp.swapaxes(cotangent, 0, 1), jnp.swapaxes(activations, 0, 1)
    act = pltpu.with_memory_space_constraint(act, pltpu.HBM)
    rows, lon_a, lon_b, wide_a, wide_b = haloes(own, place)
    lat_a = lax.ppermute(wide_a, AXES, LAT_A)
    lat_b = lax.ppermute(wide_b, AXES, LAT_B)
    tiles, cells = prepared(place, basis, reach, act, wide_a)
    f, send = stencil(place, tiles, rows, lon_a, lon_b, lat_a, lat_b, cells)
    got = lax.ppermute(send, AXES, SIBLING)
    mine = own_part(place, f, cells)
    half = (mine + got.astype(F32)).astype(BF16)
    weight = pltpu.with_memory_space_constraint(weight, pltpu.HBM)
    grad_input = input_gradient(f, weight)
    part = summed(half.reshape(-1, CHANNELS), 32, BLOCK).astype(BF16)
    part, grad_input = lax.optimization_barrier((part, grad_input))
    others = [lax.ppermute(part, AXES, along_z(m)).astype(F32) for m in (2, 6, 4)]
    norm_factor = float(ROWS * COLS * LAT * LON) ** (-0.5)
    part = (part.astype(F32) + others[0]) + (others[1] + others[2])
    part = (part * norm_factor).astype(BF16)
    parts = lax.all_to_all(jnp.broadcast_to(part, (32, *part.shape)), BLOCK, 0, 0, tiled=True)
    mine = parts.reshape(2, CHANNELS, CHANNELS)
    theirs = lax.ppermute(mine, AXES, SIBLING)
    grad_weight = put_half(place, mine, False)
    (grad_weight,) = put_half(place, theirs, True, grad_weight)
    return jnp.swapaxes(grad_input, 0, 1), grad_weight


def solution(mesh):
    finer = Mesh(mesh.devices.reshape(4, 2, 2, 2, 4, 2), AXES)
    cells = P(("y", "xh", "core"), ("xl", "zh", "zl"), None)
    return jax.shard_map(
        on_device, mesh=finer, in_specs=(cells, cells, P(), P(), P()), out_specs=(cells, P()), check_vma=False
    )
```

```python
import functools

import jax
import jax.numpy as jnp
from jax import lax
from jax.experimental import pallas as pl
from jax.experimental.pallas import tpu as pltpu
from jax.sharding import Mesh, PartitionSpec as P

ROWS, COLS, REACH = 16, 90, 16
PAD, HALF, SPAN, WIDE = 96, 48, 80, 128
DEPTH = 256
CHANNELS, FILTERS, TAPS = 512, 4, 3
AXES = ("y", "xh", "core", "xl", "zh", "zl")
BLOCK = ("y", "xh", "xl", "zl")
LAT, LON = 16, 16
MIB = 1024 * 1024
BF16, F32 = jnp.bfloat16, jnp.float32


def turned(block):
    return jnp.swapaxes(block, 0, 1)


def local(kernel, name, shapes, inputs, scratch=(), spaces=None, aliases=None, mib=16, cost=None):
    spaces = spaces or {}
    spec = lambda i: pl.BlockSpec(memory_space=spaces.get(i, pltpu.VMEM))
    n = len(inputs)
    return pl.pallas_call(
        kernel,
        in_specs=[pl.BlockSpec(memory_space=pltpu.SMEM)] + [spec(i) for i in range(1, n)],
        out_specs=[spec(n + i) for i in range(len(shapes))],
        out_shape=[jax.ShapeDtypeStruct(shape, BF16) for shape in shapes],
        scratch_shapes=list(scratch),
        input_output_aliases=aliases or {},
        compiler_params=pltpu.CompilerParams(vmem_limit_bytes=mib * MIB),
        cost_estimate=cost and pl.CostEstimate(flops=cost, bytes_accessed=2_000_000, transcendentals=0),
        name=name,
    )(*inputs)


def edges_kernel(place, own, slab_a, slab_b, edge_a, edge_b):
    even = place[1] == 0
    west, east = own[:REACH], own[COLS - REACH :]
    slab_a[...] = jnp.where(even, east, west)
    slab_b[...] = jnp.where(even, west, east)
    for slab, edge in ((slab_a, edge_a), (slab_b, edge_b)):
        block = turned(slab[...])
        edge[0], edge[1] = block[0], block[ROWS - 1]


def chunks():
    return [(b, 16 * b, min(16, COLS - 16 * b)) for b in range(PAD // 16)]


def fetches(source, target, sems):
    copies = [
        pltpu.make_async_copy(source.at[pl.ds(left, n)], target.at[pl.ds(left, n)], sems.at[b]) for b, left, n in chunks()
    ]
    for copy in copies:
        copy.start()
    return copies


def turned_chunk(block):
    if block.shape[0] < 16:
        block = jnp.concatenate([block, jnp.zeros((16 - block.shape[0], ROWS, CHANNELS), BF16)])
    return turned(block)


def turn_kernel(place, own, _, rows, middle, buffer, sems):
    copies = fetches(own, buffer, sems)
    for b, left, n in chunks():
        copies[b].wait()
        block = turned_chunk(buffer[left : left + n])
        rows[:, left : left + 16, :] = block
        middle[0, left : left + 16] = block[0]
        middle[1, left : left + 16] = block[ROWS - 1]


def widen_kernel(place, middle, got_a, got_b, wide_a, wide_b):
    even, first = place[1] == 0, place[0] == 0
    left = jnp.where(even, got_b[...], got_a[...])
    right = jnp.where(even, got_a[...], got_b[...])
    for wide, is_last in ((wide_a, first), (wide_b, jnp.logical_not(first))):
        pick = lambda x: jnp.where(is_last, x[1], x[0])
        wide[COLS + REACH :] = jnp.zeros((WIDE - COLS - REACH, CHANNELS), BF16)
        wide[:REACH] = pick(left)
        wide[REACH : COLS + REACH] = pick(middle)[:COLS]
        wide[COLS + REACH : COLS + 2 * REACH] = pick(right)


LEAD = 8


def prepare_kernel(place, basis, reach, act, _, tiles, cells, placed, buffer, sems):
    copies = fetches(act, buffer, sems)
    length = basis.shape[1] * FILTERS
    lats = basis.shape[3]
    offset = lax.broadcasted_iota(jnp.int32, (length, lats), 0) // FILTERS
    inside = jnp.abs(offset - REACH) <= reach[...]
    row = lax.broadcasted_iota(jnp.int32, (length, FILTERS * DEPTH), 0)
    col = lax.broadcasted_iota(jnp.int32, (length, FILTERS * DEPTH), 1)
    gap = jnp.where(row % FILTERS == col // DEPTH, col % DEPTH + row // FILTERS - 2 * REACH, -1)

    def put(t, q, lat):
        taps = jnp.where(inside, basis[t].astype(F32).reshape(length, lats), 0.0)[:, lat].astype(BF16)
        ones = jnp.where(gap == SPAN * q, 1.0, 0.0).astype(BF16)
        return lax.dot_general(taps, ones, (((0,), (0,)), ((), ())), preferred_element_type=F32)

    for q in range(TAPS):
        placed[q, LEAD : LEAD + lats, :] = put(TAPS - 1 - q, q, slice(None))
    placed[0, LEAD - 1 : LEAD, :] = put(0, 0, slice(0, 128))[:1]
    placed[2, LEAD + lats : LEAD + lats + 1, :] = put(2, 2, slice(lats - 128, lats))[127:]
    start = place[2] * ROWS + LEAD - 1
    for r in range(ROWS):
        for k in range(FILTERS):
            lanes = pl.ds(k * DEPTH, DEPTH)
            taps = [placed[q, pl.ds(start + r + q, 1), lanes] for q in range(TAPS)]
            band = jnp.broadcast_to(taps[0] + taps[1] + taps[2], (HALF, DEPTH))
            tiles[r, k * HALF : (k + 1) * HALF, :] = pltpu.roll(band, 0, 1, stride=1, stride_axis=0).astype(BF16)
    for b, left, n in chunks():
        copies[b].wait()
        cells[:, left : left + 16, :] = turned_chunk(buffer[left : left + n])


GROUP = 4
STEPS = ROWS // GROUP


def outer(f, cells):
    f = f.reshape(ROWS * PAD, CHANNELS)
    cells = cells.reshape(ROWS * PAD, CHANNELS)
    return lax.dot_general(f, cells, (((0,), (0,)), ((), ())), preferred_element_type=F32)


def stencil_kernel(place, tiles, rows, lon_b, lon_a, lat_a, lat_b, cells_ref, f_out, send, low, high, held, cells, sem, f_sems):
    step = pl.program_id(0)
    stores = [
        pltpu.make_async_copy(held.at[:, pl.ds(GROUP * i, GROUP)], f_out.at[:, pl.ds(GROUP * i, GROUP)], f_sems.at[i])
        for i in range(STEPS)
    ]
    copy = pltpu.make_async_copy(cells_ref, cells, sem)

    @pl.when(step == 0)
    def _():
        copy.start()
        even, first = place[1] == 0, place[0] == 0
        inner = slice(1, ROWS + 1)
        low[inner, :REACH, :] = turned(jnp.where(even, lon_b[...], lon_a[...]))
        low[inner, REACH:, :] = rows[:, : SPAN - REACH, :]
        high[inner, : PAD - 32, :] = rows[:, 32:PAD, :]
        high[inner, PAD - 32 :, :] = jnp.zeros((ROWS, SPAN + 32 - PAD, CHANNELS), BF16)
        right = turned(jnp.where(even, lon_a[...], lon_b[...]))
        for r in range(ROWS):
            high[r + 1, COLS - 32 : COLS - 32 + REACH, :] = right[r]
        before = jnp.where(first, lat_b[...], lat_a[...])
        after = jnp.where(first, lat_a[...], lat_b[...])
        low[0], low[ROWS + 1] = before[:SPAN], after[:SPAN]
        high[0], high[ROWS + 1] = before[HALF:], after[HALF:]

    @pl.when(step < STEPS)
    def _():
        rest = jnp.zeros((DEPTH - TAPS * SPAN, CHANNELS), BF16)
        for j in range(GROUP):
            r = step * GROUP + j
            for h, source in enumerate((low, high)):
                taken = source[pl.ds(r, TAPS)].reshape(TAPS * SPAN, CHANNELS)
                taken = jnp.concatenate([taken, rest])
                f = jnp.dot(tiles[j], taken, preferred_element_type=F32).astype(BF16)
                f = f.reshape(FILTERS, HALF, CHANNELS)
                held[:, r, h * HALF : (h + 1) * HALF, :] = f

    for i, store in enumerate(stores):
        pl.when(step == i)(store.start)

    @pl.when(step == STEPS)
    def _():
        copy.wait()

    @pl.when(step >= STEPS)
    def _():
        k = 2 * (1 - place[0]) + step - STEPS
        send[0] = outer(held[k], cells[...]).astype(BF16)

    @pl.when(step == STEPS + 1)
    def _():
        for store in stores:
            store.wait()


def stencil(place, tiles, rows, lon_a, lon_b, lat_a, lat_b, cells):
    whole = lambda a: pl.BlockSpec(a.shape, lambda i, c: (0,) * a.ndim)
    return pl.pallas_call(
        stencil_kernel,
        grid_spec=pltpu.PrefetchScalarGridSpec(
            num_scalar_prefetch=1,
            grid=(STEPS + 2,),
            in_specs=[
                pl.BlockSpec((GROUP, FILTERS * HALF, DEPTH), lambda i, c: (jnp.minimum(i, STEPS - 1), 0, 0)),
                *[whole(a) for a in (rows, lon_b, lon_a, lat_a, lat_b)],
                pl.BlockSpec(memory_space=pl.ANY),
            ],
            out_specs=[
                pl.BlockSpec(memory_space=pltpu.HBM),
                pl.BlockSpec((1, CHANNELS, CHANNELS), lambda i, c: (jnp.maximum(i - STEPS, 0), 0, 0)),
            ],
            scratch_shapes=[
                pltpu.VMEM((ROWS + 2, SPAN, CHANNELS), BF16),
                pltpu.VMEM((ROWS + 2, SPAN, CHANNELS), BF16),
                pltpu.VMEM((FILTERS, ROWS, PAD, CHANNELS), BF16),
                pltpu.VMEM((ROWS, PAD, CHANNELS), BF16),
                pltpu.SemaphoreType.DMA(()),
                pltpu.SemaphoreType.DMA((STEPS,)),
            ],
        ),
        out_shape=[
            jax.ShapeDtypeStruct((FILTERS, ROWS, PAD, CHANNELS), BF16),
            jax.ShapeDtypeStruct((2, CHANNELS, CHANNELS), BF16),
        ],
        compiler_params=pltpu.CompilerParams(vmem_limit_bytes=30 * MIB),
        name="stencil",
    )(place, tiles, rows, lon_b, lon_a, lat_a, lat_b, cells)


def own_part_kernel(place, f_hbm, cells_ref, mine, f, cells, sems):
    copies = [pltpu.make_async_copy(f_hbm.at[2 * place[0] + j], f.at[j], sems.at[j]) for j in range(2)]
    copies.append(pltpu.make_async_copy(cells_ref, cells, sems.at[2]))
    for copy in (copies[2], copies[0], copies[1]):
        copy.start()
    copies[2].wait()
    for j in range(2):
        copies[j].wait()
        mine[j] = outer(f[j], cells[...])


def spec(space):
    return pl.BlockSpec(memory_space=space)


def own_part(place, f, cells):
    return pl.pallas_call(
        own_part_kernel,
        in_specs=[spec(pltpu.SMEM), spec(pl.ANY), spec(pl.ANY)],
        out_specs=spec(pltpu.VMEM),
        out_shape=jax.ShapeDtypeStruct((2, CHANNELS, CHANNELS), F32),
        scratch_shapes=[
            pltpu.VMEM((2, ROWS, PAD, CHANNELS), BF16),
            pltpu.VMEM((ROWS, PAD, CHANNELS), BF16),
            pltpu.SemaphoreType.DMA((3,)),
        ],
        compiler_params=pltpu.CompilerParams(vmem_limit_bytes=16 * MIB),
        cost_estimate=pl.CostEstimate(flops=4 * ROWS * PAD * CHANNELS**2, bytes_accessed=6_000_000, transcendentals=0),
        name="own_part",
    )(place, f, cells)


SLAB = 32
SLABS = PAD // SLAB


def input_kernel(f_hbm, weight_hbm, out, weight, f, stage, weight_sems, f_sems, out_sems):
    loads = [pltpu.make_async_copy(weight_hbm.at[k], weight.at[k], weight_sems.at[k]) for k in range(FILTERS)]
    slabs = []
    for j in range(SLABS):
        at = pl.ds(SLAB * j, SLAB)
        slabs.append([pltpu.make_async_copy(f_hbm.at[k, :, at], f.at[k, :, at], f_sems.at[j, k]) for k in range(FILTERS)])
    for k in range(FILTERS):
        slabs[0][k].start()
        loads[k].start()
    for slab in slabs[1:]:
        for copy in slab:
            copy.start()
    stores = []
    for j in range(SLABS):
        left = SLAB * j
        cols = min(SLAB, COLS - left)
        total = 0.0
        for k in range(FILTERS):
            slabs[j][k].wait()
            if j == 0:
                loads[k].wait()
            taken = f[k, :, left : left + SLAB, :].reshape(ROWS * SLAB, CHANNELS)
            total += jnp.dot(taken, weight[k], preferred_element_type=F32)
        total = total.astype(BF16).reshape(ROWS, SLAB, CHANNELS)
        for b in range(SLAB // 16):
            stage[j, 16 * b : 16 * (b + 1)] = turned(total[:, 16 * b : 16 * (b + 1)])
        store = pltpu.make_async_copy(stage.at[j, pl.ds(0, cols)], out.at[pl.ds(left, cols)], out_sems.at[j])
        store.start()
        stores.append(store)
    for store in stores:
        store.wait()


def input_gradient(f, weight):
    flops = 2 * ROWS * PAD * FILTERS * CHANNELS * CHANNELS
    return pl.pallas_call(
        input_kernel,
        in_specs=[spec(pl.ANY), spec(pltpu.HBM)],
        out_specs=spec(pl.ANY),
        out_shape=jax.ShapeDtypeStruct((COLS, ROWS, CHANNELS), BF16),
        scratch_shapes=[
            pltpu.VMEM((FILTERS, CHANNELS, CHANNELS), BF16),
            pltpu.VMEM((FILTERS, ROWS, PAD, CHANNELS), BF16),
            pltpu.VMEM((SLABS, SLAB, ROWS, CHANNELS), BF16),
            pltpu.SemaphoreType.DMA((FILTERS,)),
            pltpu.SemaphoreType.DMA((SLABS, FILTERS)),
            pltpu.SemaphoreType.DMA((SLABS,)),
        ],
        compiler_params=pltpu.CompilerParams(vmem_limit_bytes=20 * MIB),
        cost_estimate=pl.CostEstimate(flops=flops, bytes_accessed=10_000_000, transcendentals=0),
        name="input_gradient",
    )(f, weight)


def put_half_kernel(flip, place, half, *rest):
    out, sems = rest[-2:]
    start = 2 * (1 - place[0] if flip else place[0])
    part = CHANNELS // 4
    copies = [
        pltpu.make_async_copy(half.at[:, pl.ds(i * part, part)], out.at[pl.ds(start, 2), pl.ds(i * part, part)], sems.at[i])
        for i in range(4)
    ]
    for copy in copies:
        copy.start()
    for copy in copies:
        copy.wait()


def put_half(place, half, flip, done=()):
    inputs = [place, half, *done]
    spaces = {i: pl.ANY for i in range(1, len(inputs) + 1)}
    return local(
        functools.partial(put_half_kernel, flip), "put_half", [(FILTERS, CHANNELS, CHANNELS)], inputs,
        [pltpu.SemaphoreType.DMA((4,))], spaces, {2: 0} if done else {},
    )


def device(lat, lon):
    return lat * LON + lon % LON


def route(target):
    return [(device(a, b), device(*target(a, b))) for a in range(LAT) for b in range(LON)]


def lat_b_partner(a, b):
    if a in (0, LAT - 1):
        return a, b + LON // 2
    return (a + 1 if a % 2 else a - 1), b


LON_A = route(lambda a, b: (a, b ^ 1))
LON_B = route(lambda a, b: (a, b + 1 if b % 2 else b - 1))
LAT_A = route(lambda a, b: (a ^ 1, b))
LAT_B = route(lat_b_partner)
SIBLING = LAT_A


def along_z(mask):
    return route(lambda a, b: (a, b ^ mask))


def haloes(own, place):
    slab, edge, wide = (REACH, ROWS, CHANNELS), (2, REACH, CHANNELS), (WIDE, CHANNELS)
    slab_a, slab_b, edge_a, edge_b = local(edges_kernel, "edges", [slab, slab, edge, edge], [place, own])
    rows, middle = local(
        turn_kernel, "turn", [(ROWS, PAD, CHANNELS), (2, PAD, CHANNELS)], [place, own, edge_b],
        [pltpu.VMEM(own.shape, BF16), pltpu.SemaphoreType.DMA((PAD // 16,))], {1: pltpu.HBM, 2: pl.ANY}, cost=4_000_000_000,
    )
    edge_a = lax.ppermute(edge_a, AXES, LON_A)
    edge_b = lax.ppermute(edge_b, AXES, LON_B)
    lon_a = lax.ppermute(slab_a, AXES, LON_A)
    lon_b = lax.ppermute(slab_b, AXES, LON_B)
    wide_a, wide_b = local(widen_kernel, "widen", [wide, wide], [place, middle, edge_a, edge_b])
    return rows, lon_a, lon_b, wide_a, wide_b


def prepared(place, basis, reach, act, after):
    lats = basis.shape[3]
    basis = jnp.transpose(basis, (1, 2, 0, 3))
    scratch = [
        pltpu.VMEM((TAPS, lats + 2 * LEAD, FILTERS * DEPTH), F32),
        pltpu.VMEM(act.shape, BF16),
        pltpu.SemaphoreType.DMA((PAD // 16,)),
    ]
    shapes = [(ROWS, FILTERS * HALF, DEPTH), (ROWS, PAD, CHANNELS)]
    inputs = [place, basis, reach.reshape(1, lats), act, after]
    return local(prepare_kernel, "prepare", shapes, inputs, scratch, {3: pltpu.HBM, 4: pl.ANY}, cost=1_000_000_000)


def summed(parts, groups, axes):
    parts = lax.all_to_all(parts.reshape(groups, -1, CHANNELS), axes, 0, 0, tiled=True)
    return jnp.sum(parts.astype(F32), axis=0)


def on_device(cotangent, activations, weight, basis, reach):
    band = lax.axis_index(("y", "xh", "core")).astype(jnp.int32)
    core = lax.axis_index("core").astype(jnp.int32)
    odd = lax.axis_index("zl").astype(jnp.int32)
    place = jnp.stack([core, odd, band])
    own, act = jnp.swapaxes(cotangent, 0, 1), jnp.swapaxes(activations, 0, 1)
    act = pltpu.with_memory_space_constraint(act, pltpu.HBM)
    rows, lon_a, lon_b, wide_a, wide_b = haloes(own, place)
    lat_a = lax.ppermute(wide_a, AXES, LAT_A)
    lat_b = lax.ppermute(wide_b, AXES, LAT_B)
    tiles, cells = prepared(place, basis, reach, act, wide_a)
    f, send = stencil(place, tiles, rows, lon_a, lon_b, lat_a, lat_b, cells)
    got = lax.ppermute(send, AXES, SIBLING)
    mine = own_part(place, f, cells)
    half = (mine + got.astype(F32)).astype(BF16)
    weight = pltpu.with_memory_space_constraint(weight, pltpu.HBM)
    grad_input = input_gradient(f, weight)
    part = summed(half.reshape(-1, CHANNELS), 32, BLOCK).astype(BF16)
    part, grad_input = lax.optimization_barrier((part, grad_input))
    others = [lax.ppermute(part, AXES, along_z(m)).astype(F32) for m in (2, 6, 4)]
    norm_factor = float(ROWS * COLS * LAT * LON) ** (-0.5)
    part = (part.astype(F32) + others[0]) + (others[1] + others[2])
    part = (part * norm_factor).astype(BF16)
    parts = lax.all_to_all(jnp.broadcast_to(part, (32, *part.shape)), BLOCK, 0, 0, tiled=True)
    mine = parts.reshape(2, CHANNELS, CHANNELS)
    theirs = lax.ppermute(mine, AXES, SIBLING)
    grad_weight = put_half(place, mine, False)
    (grad_weight,) = put_half(place, theirs, True, grad_weight)
    return jnp.swapaxes(grad_input, 0, 1), grad_weight


def solution(mesh):
    finer = Mesh(mesh.devices.reshape(4, 2, 2, 2, 4, 2), AXES)
    cells = P(("y", "xh", "core"), ("xl", "zh", "zl"), None)
    return jax.shard_map(
        on_device, mesh=finer, in_specs=(cells, cells, P(), P(), P()), out_specs=(cells, P()), check_vma=False
    )
```

```python
import functools

import jax
import jax.numpy as jnp
from jax import lax
from jax.experimental import pallas as pl
from jax.experimental.pallas import tpu as pltpu
from jax.sharding import Mesh, PartitionSpec as P

ROWS, COLS, REACH = 16, 90, 16
PAD, PART, SPAN, WIDE = 96, 32, 64, 128
DEPTH = 4 * SPAN
PARTS = PAD // PART
CHANNELS, FILTERS, TAPS = 512, 4, 3
AXES = ("y", "xh", "core", "xl", "zh", "zl")
BLOCK = ("y", "xh", "xl", "zl")
LAT, LON = 16, 16
MIB = 1024 * 1024
BF16, F32 = jnp.bfloat16, jnp.float32


def turned(block):
    return jnp.swapaxes(block, 0, 1)


def local(kernel, name, shapes, inputs, scratch=(), spaces=None, aliases=None, mib=16, cost=None):
    spaces = spaces or {}
    spec = lambda i: pl.BlockSpec(memory_space=spaces.get(i, pltpu.VMEM))
    n = len(inputs)
    return pl.pallas_call(
        kernel,
        in_specs=[pl.BlockSpec(memory_space=pltpu.SMEM)] + [spec(i) for i in range(1, n)],
        out_specs=[spec(n + i) for i in range(len(shapes))],
        out_shape=[jax.ShapeDtypeStruct(shape, BF16) for shape in shapes],
        scratch_shapes=list(scratch),
        input_output_aliases=aliases or {},
        compiler_params=pltpu.CompilerParams(vmem_limit_bytes=mib * MIB),
        cost_estimate=cost and pl.CostEstimate(flops=cost, bytes_accessed=2_000_000, transcendentals=0),
        name=name,
    )(*inputs)


def edges_kernel(place, own, slab_a, slab_b, edge_a, edge_b, middle):
    even = place[1] == 0
    west, east = own[:REACH], own[COLS - REACH :]
    slab_a[...] = jnp.where(even, east, west)
    slab_b[...] = jnp.where(even, west, east)
    for slab, edge in ((slab_a, edge_a), (slab_b, edge_b)):
        block = turned(slab[...])
        edge[0], edge[1] = block[0], block[ROWS - 1]
    for b, left, n in chunks():
        block = turned_chunk(own[left : left + n])
        middle[0, left : left + 16] = block[0]
        middle[1, left : left + 16] = block[ROWS - 1]


def chunks():
    return [(b, 16 * b, min(16, COLS - 16 * b)) for b in range(PAD // 16)]


def fetches(source, target, sems):
    copies = [
        pltpu.make_async_copy(source.at[pl.ds(left, n)], target.at[pl.ds(left, n)], sems.at[b]) for b, left, n in chunks()
    ]
    for copy in copies:
        copy.start()
    return copies


def turned_chunk(block):
    if block.shape[0] < 16:
        block = jnp.concatenate([block, jnp.zeros((16 - block.shape[0], ROWS, CHANNELS), BF16)])
    return turned(block)


def ordered_kernel(place, middle, _, out):
    first = place[0] == 0
    out[0] = jnp.where(first, middle[1], middle[0])
    out[1] = jnp.where(first, middle[0], middle[1])


def widen_kernel(place, middle, got_a, got_b, wide_a, wide_b):
    even, first = place[1] == 0, place[0] == 0
    left = jnp.where(even, got_b[...], got_a[...])
    right = jnp.where(even, got_a[...], got_b[...])
    for i, (wide, is_last) in enumerate(((wide_a, first), (wide_b, jnp.logical_not(first)))):
        pick = lambda x: jnp.where(is_last, x[1], x[0])
        wide[COLS + REACH :] = jnp.zeros((WIDE - COLS - REACH, CHANNELS), BF16)
        wide[:REACH] = pick(left)
        wide[REACH : COLS + REACH] = middle[i, :COLS]
        wide[COLS + REACH : COLS + 2 * REACH] = pick(right)


LEAD = 8


def prepare_kernel(place, basis, reach, act, own, _, tiles, cells, rows, placed, buffer, sems):
    copies = fetches(act, buffer, sems)
    length = basis.shape[1] * FILTERS
    lats = basis.shape[3]
    offset = lax.broadcasted_iota(jnp.int32, (length, lats), 0) // FILTERS
    inside = jnp.abs(offset - REACH) <= reach[...]
    row = lax.broadcasted_iota(jnp.int32, (length, FILTERS * DEPTH), 0)
    col = lax.broadcasted_iota(jnp.int32, (length, FILTERS * DEPTH), 1)
    gap = jnp.where(row % FILTERS == col // DEPTH, col % DEPTH + row // FILTERS - 2 * REACH, -1)

    def put(t, q, lat):
        taps = jnp.where(inside, basis[t].astype(F32).reshape(length, lats), 0.0)[:, lat].astype(BF16)
        ones = jnp.where(gap == SPAN * q, 1.0, 0.0).astype(BF16)
        return lax.dot_general(taps, ones, (((0,), (0,)), ((), ())), preferred_element_type=F32)

    for q in range(TAPS):
        placed[q, LEAD : LEAD + lats, :] = put(TAPS - 1 - q, q, slice(None))
    placed[0, LEAD - 1 : LEAD, :] = put(0, 0, slice(0, 128))[:1]
    placed[2, LEAD + lats : LEAD + lats + 1, :] = put(2, 2, slice(lats - 128, lats))[127:]
    start = place[2] * ROWS + LEAD - 1
    for r in range(ROWS):
        for k in range(FILTERS):
            lanes = pl.ds(k * DEPTH, DEPTH)
            taps = [placed[q, pl.ds(start + r + q, 1), lanes] for q in range(TAPS)]
            band = jnp.broadcast_to(taps[0] + taps[1] + taps[2], (PART, DEPTH))
            band = pltpu.roll(band, SPAN * (r % 2), 1, stride=1, stride_axis=0)
            first = (r % 2) * FILTERS * PART + k * PART
            tiles[r // 2, first : first + PART, :] = band.astype(BF16)
    for b, left, n in chunks():
        copies[b].wait()
        cells[:, left : left + 16, :] = turned_chunk(buffer[left : left + n])
        rows[:, left : left + 16, :] = turned_chunk(own[left : left + n])


GROUP = 8
STEPS = ROWS // GROUP


def outer(f, cells):
    f = f.reshape(ROWS * PAD, CHANNELS)
    cells = cells.reshape(ROWS * PAD, CHANNELS)
    return lax.dot_general(f, cells, (((0,), (0,)), ((), ())), preferred_element_type=F32)


def stencil_kernel(place, tiles, rows, lon_b, lon_a, lat_a, lat_b, cells_ref, f_out, send, spans, held, cells, sem, f_sems):
    step = pl.program_id(0)
    stores = [
        pltpu.make_async_copy(held.at[:, pl.ds(GROUP * i, GROUP)], f_out.at[:, pl.ds(GROUP * i, GROUP)], f_sems.at[i])
        for i in range(STEPS)
    ]
    copy = pltpu.make_async_copy(cells_ref, cells, sem)

    @pl.when(step == 0)
    def _():
        copy.start()
        even, first = place[1] == 0, place[0] == 0
        inner = slice(1, ROWS + 1)
        spans[0, inner, :REACH, :] = turned(jnp.where(even, lon_b[...], lon_a[...]))
        spans[0, inner, REACH:, :] = rows[:, :48, :]
        spans[1, inner, :, :] = rows[:, 16:80, :]
        spans[2, inner, :48, :] = rows[:, 48:PAD, :]
        spans[2, inner, 48:, :] = jnp.zeros((ROWS, SPAN - 48, CHANNELS), BF16)
        right = turned(jnp.where(even, lon_a[...], lon_b[...]))
        for r in range(ROWS):
            spans[2, r + 1, COLS - 48 : COLS - 48 + REACH, :] = right[r]
        before = jnp.where(first, lat_b[...], lat_a[...])
        after = jnp.where(first, lat_a[...], lat_b[...])
        for h in range(PARTS):
            spans[h, 0] = before[PART * h : PART * h + SPAN]
            spans[h, ROWS + 1] = after[PART * h : PART * h + SPAN]

    @pl.when(step < STEPS)
    def _():
        for pair in range(GROUP // 2):
            r = step * GROUP + 2 * pair
            for h in range(PARTS):
                taken = spans[h, pl.ds(r, 4)].reshape(DEPTH, CHANNELS)
                f = jnp.dot(tiles[pair], taken, preferred_element_type=F32).astype(BF16)
                f = f.reshape(2, FILTERS, PART, CHANNELS)
                for j in range(2):
                    held[:, r + j, h * PART : (h + 1) * PART, :] = f[j]

    for i, store in enumerate(stores):
        pl.when(step == i)(store.start)

    @pl.when(step == STEPS)
    def _():
        copy.wait()
        for j in range(2):
            send[j] = outer(held[2 * (1 - place[0]) + j], cells[...]).astype(BF16)
        for store in stores:
            store.wait()


def stencil(place, tiles, rows, lon_a, lon_b, lat_a, lat_b, cells):
    whole = lambda a: pl.BlockSpec(a.shape, lambda i, c: (0,) * a.ndim)
    return pl.pallas_call(
        stencil_kernel,
        grid_spec=pltpu.PrefetchScalarGridSpec(
            num_scalar_prefetch=1,
            grid=(STEPS + 1,),
            in_specs=[
                pl.BlockSpec((GROUP // 2, 2 * FILTERS * PART, DEPTH), lambda i, c: (jnp.minimum(i, STEPS - 1), 0, 0)),
                *[whole(a) for a in (rows, lon_b, lon_a, lat_a, lat_b)],
                pl.BlockSpec(memory_space=pl.ANY),
            ],
            out_specs=[
                pl.BlockSpec(memory_space=pltpu.HBM),
                pl.BlockSpec((2, CHANNELS, CHANNELS), lambda i, c: (0, 0, 0)),
            ],
            scratch_shapes=[
                pltpu.VMEM((PARTS, ROWS + 2, SPAN, CHANNELS), BF16),
                pltpu.VMEM((FILTERS, ROWS, PAD, CHANNELS), BF16),
                pltpu.VMEM((ROWS, PAD, CHANNELS), BF16),
                pltpu.SemaphoreType.DMA(()),
                pltpu.SemaphoreType.DMA((STEPS,)),
            ],
        ),
        out_shape=[
            jax.ShapeDtypeStruct((FILTERS, ROWS, PAD, CHANNELS), BF16),
            jax.ShapeDtypeStruct((2, CHANNELS, CHANNELS), BF16),
        ],
        compiler_params=pltpu.CompilerParams(vmem_limit_bytes=30 * MIB),
        name="stencil",
    )(place, tiles, rows, lon_b, lon_a, lat_a, lat_b, cells)


def own_part_kernel(place, f_hbm, cells_ref, mine, f, cells, sems):
    copies = [pltpu.make_async_copy(f_hbm.at[2 * place[0] + j], f.at[j], sems.at[j]) for j in range(2)]
    copies.append(pltpu.make_async_copy(cells_ref, cells, sems.at[2]))
    for copy in (copies[2], copies[0], copies[1]):
        copy.start()
    copies[2].wait()
    for j in range(2):
        copies[j].wait()
        mine[j] = outer(f[j], cells[...])


def spec(space):
    return pl.BlockSpec(memory_space=space)


def own_part(place, f, cells):
    return pl.pallas_call(
        own_part_kernel,
        in_specs=[spec(pltpu.SMEM), spec(pl.ANY), spec(pl.ANY)],
        out_specs=spec(pltpu.VMEM),
        out_shape=jax.ShapeDtypeStruct((2, CHANNELS, CHANNELS), F32),
        scratch_shapes=[
            pltpu.VMEM((2, ROWS, PAD, CHANNELS), BF16),
            pltpu.VMEM((ROWS, PAD, CHANNELS), BF16),
            pltpu.SemaphoreType.DMA((3,)),
        ],
        compiler_params=pltpu.CompilerParams(vmem_limit_bytes=16 * MIB),
        cost_estimate=pl.CostEstimate(flops=4 * ROWS * PAD * CHANNELS**2, bytes_accessed=6_000_000, transcendentals=0),
        name="own_part",
    )(place, f, cells)


SLAB = 32
SLABS = PAD // SLAB


def input_kernel(f_hbm, weight_hbm, out, weight, f, stage, weight_sems, f_sems, out_sems):
    loads = [pltpu.make_async_copy(weight_hbm.at[k], weight.at[k], weight_sems.at[k]) for k in range(FILTERS)]
    slabs = []
    for j in range(SLABS):
        at = pl.ds(SLAB * j, SLAB)
        slabs.append([pltpu.make_async_copy(f_hbm.at[k, :, at], f.at[k, :, at], f_sems.at[j, k]) for k in range(FILTERS)])
    for k in range(FILTERS):
        slabs[0][k].start()
        loads[k].start()
    for slab in slabs[1:]:
        for copy in slab:
            copy.start()
    stores = []
    for j in range(SLABS):
        left = SLAB * j
        cols = min(SLAB, COLS - left)
        total = 0.0
        for k in range(FILTERS):
            slabs[j][k].wait()
            if j == 0:
                loads[k].wait()
            taken = f[k, :, left : left + SLAB, :].reshape(ROWS * SLAB, CHANNELS)
            total += jnp.dot(taken, weight[k], preferred_element_type=F32)
        total = total.astype(BF16).reshape(ROWS, SLAB, CHANNELS)
        for b in range(SLAB // 16):
            stage[j, 16 * b : 16 * (b + 1)] = turned(total[:, 16 * b : 16 * (b + 1)])
        store = pltpu.make_async_copy(stage.at[j, pl.ds(0, cols)], out.at[pl.ds(left, cols)], out_sems.at[j])
        store.start()
        stores.append(store)
    for store in stores:
        store.wait()


def input_gradient(f, weight):
    flops = 2 * ROWS * PAD * FILTERS * CHANNELS * CHANNELS
    return pl.pallas_call(
        input_kernel,
        in_specs=[spec(pl.ANY), spec(pltpu.HBM)],
        out_specs=spec(pl.ANY),
        out_shape=jax.ShapeDtypeStruct((COLS, ROWS, CHANNELS), BF16),
        scratch_shapes=[
            pltpu.VMEM((FILTERS, CHANNELS, CHANNELS), BF16),
            pltpu.VMEM((FILTERS, ROWS, PAD, CHANNELS), BF16),
            pltpu.VMEM((SLABS, SLAB, ROWS, CHANNELS), BF16),
            pltpu.SemaphoreType.DMA((FILTERS,)),
            pltpu.SemaphoreType.DMA((SLABS, FILTERS)),
            pltpu.SemaphoreType.DMA((SLABS,)),
        ],
        compiler_params=pltpu.CompilerParams(vmem_limit_bytes=20 * MIB),
        cost_estimate=pl.CostEstimate(flops=flops, bytes_accessed=10_000_000, transcendentals=0),
        name="input_gradient",
    )(f, weight)


def put_half_kernel(flip, place, half, *rest):
    out, sems = rest[-2:]
    start = 2 * (1 - place[0] if flip else place[0])
    part = CHANNELS // 4
    copies = [
        pltpu.make_async_copy(half.at[:, pl.ds(i * part, part)], out.at[pl.ds(start, 2), pl.ds(i * part, part)], sems.at[i])
        for i in range(4)
    ]
    for copy in copies:
        copy.start()
    for copy in copies:
        copy.wait()


def put_half(place, half, flip, done=()):
    inputs = [place, half, *done]
    spaces = {i: pl.ANY for i in range(1, len(inputs) + 1)}
    return local(
        functools.partial(put_half_kernel, flip), "put_half", [(FILTERS, CHANNELS, CHANNELS)], inputs,
        [pltpu.SemaphoreType.DMA((4,))], spaces, {2: 0} if done else {},
    )


def device(lat, lon):
    return lat * LON + lon % LON


def route(target):
    return [(device(a, b), device(*target(a, b))) for a in range(LAT) for b in range(LON)]


def lat_b_partner(a, b):
    if a in (0, LAT - 1):
        return a, b + LON // 2
    return (a + 1 if a % 2 else a - 1), b


LON_A = route(lambda a, b: (a, b ^ 1))
LON_B = route(lambda a, b: (a, b + 1 if b % 2 else b - 1))
LAT_A = route(lambda a, b: (a ^ 1, b))
LAT_B = route(lat_b_partner)
SIBLING = LAT_A


def along_z(mask):
    return route(lambda a, b: (a, b ^ mask))


def haloes(own, place):
    slab, edge, wide = (REACH, ROWS, CHANNELS), (2, REACH, CHANNELS), (WIDE, CHANNELS)
    rows = (2, PAD, CHANNELS)
    slab_a, slab_b, edge_a, edge_b, middle = local(edges_kernel, "edges", [slab, slab, edge, edge, rows], [place, own])
    (middle,) = local(ordered_kernel, "ordered", [rows], [place, middle, edge_b], spaces={2: pl.ANY}, cost=4_000_000_000)
    edge_a = lax.ppermute(edge_a, AXES, LON_A)
    edge_b = lax.ppermute(edge_b, AXES, LON_B)
    lon_a = lax.ppermute(slab_a, AXES, LON_A)
    lon_b = lax.ppermute(slab_b, AXES, LON_B)
    wide_a, wide_b = local(widen_kernel, "widen", [wide, wide], [place, middle, edge_a, edge_b])
    return lon_a, lon_b, wide_a, wide_b


def prepared(place, basis, reach, act, own, after):
    lats = basis.shape[3]
    basis = jnp.transpose(basis, (1, 2, 0, 3))
    scratch = [
        pltpu.VMEM((TAPS, lats + 2 * LEAD, FILTERS * DEPTH), F32),
        pltpu.VMEM(act.shape, BF16),
        pltpu.SemaphoreType.DMA((PAD // 16,)),
    ]
    rows = (ROWS, PAD, CHANNELS)
    shapes = [(ROWS // 2, 2 * FILTERS * PART, DEPTH), rows, rows]
    inputs = [place, basis, reach.reshape(1, lats), act, own, after]
    return local(prepare_kernel, "prepare", shapes, inputs, scratch, {3: pltpu.HBM, 5: pl.ANY}, cost=1_000_000_000)


def summed(parts, groups, axes):
    parts = lax.all_to_all(parts.reshape(groups, -1, CHANNELS), axes, 0, 0, tiled=True)
    return jnp.sum(parts.astype(F32), axis=0)


def on_device(cotangent, activations, weight, basis, reach):
    band = lax.axis_index(("y", "xh", "core")).astype(jnp.int32)
    core = lax.axis_index("core").astype(jnp.int32)
    odd = lax.axis_index("zl").astype(jnp.int32)
    place = jnp.stack([core, odd, band])
    own, act = jnp.swapaxes(cotangent, 0, 1), jnp.swapaxes(activations, 0, 1)
    act = pltpu.with_memory_space_constraint(act, pltpu.HBM)
    lon_a, lon_b, wide_a, wide_b = haloes(own, place)
    lat_a = lax.ppermute(wide_a, AXES, LAT_A)
    lat_b = lax.ppermute(wide_b, AXES, LAT_B)
    tiles, cells, rows = prepared(place, basis, reach, act, own, wide_a)
    f, send = stencil(place, tiles, rows, lon_a, lon_b, lat_a, lat_b, cells)
    got = lax.ppermute(send, AXES, SIBLING)
    mine = own_part(place, f, cells)
    half = (mine + got.astype(F32)).astype(BF16)
    weight = pltpu.with_memory_space_constraint(weight, pltpu.HBM)
    grad_input = input_gradient(f, weight)
    part = summed(half.reshape(-1, CHANNELS), 32, BLOCK).astype(BF16)
    part, grad_input = lax.optimization_barrier((part, grad_input))
    others = [lax.ppermute(part, AXES, along_z(m)).astype(F32) for m in (2, 6, 4)]
    norm_factor = float(ROWS * COLS * LAT * LON) ** (-0.5)
    part = (part.astype(F32) + others[0]) + (others[1] + others[2])
    part = (part * norm_factor).astype(BF16)
    parts = lax.all_to_all(jnp.broadcast_to(part, (32, *part.shape)), BLOCK, 0, 0, tiled=True)
    mine = parts.reshape(2, CHANNELS, CHANNELS)
    theirs = lax.ppermute(mine, AXES, SIBLING)
    grad_weight = put_half(place, mine, False)
    (grad_weight,) = put_half(place, theirs, True, grad_weight)
    return jnp.swapaxes(grad_input, 0, 1), grad_weight


def solution(mesh):
    finer = Mesh(mesh.devices.reshape(4, 2, 2, 2, 4, 2), AXES)
    cells = P(("y", "xh", "core"), ("xl", "zh", "zl"), None)
    return jax.shard_map(
        on_device, mesh=finer, in_specs=(cells, cells, P(), P(), P()), out_specs=(cells, P()), check_vma=False
    )
```

```python
import functools

import jax
import jax.numpy as jnp
from jax import lax
from jax.experimental import pallas as pl
from jax.experimental.pallas import tpu as pltpu
from jax.sharding import Mesh, PartitionSpec as P

ROWS, COLS, REACH = 16, 90, 16
PAD, PART, SPAN, WIDE = 96, 32, 64, 128
DEPTH = 4 * SPAN
PARTS = PAD // PART
CHANNELS, FILTERS, TAPS = 512, 4, 3
AXES = ("y", "xh", "core", "xl", "zh", "zl")
BLOCK = ("y", "xh", "xl", "zl")
LAT, LON = 16, 16
MIB = 1024 * 1024
BF16, F32 = jnp.bfloat16, jnp.float32


def turned(block):
    return jnp.swapaxes(block, 0, 1)


def local(kernel, name, shapes, inputs, scratch=(), spaces=None, aliases=None, mib=16, cost=None):
    spaces = spaces or {}
    spec = lambda i: pl.BlockSpec(memory_space=spaces.get(i, pltpu.VMEM))
    n = len(inputs)
    return pl.pallas_call(
        kernel,
        in_specs=[pl.BlockSpec(memory_space=pltpu.SMEM)] + [spec(i) for i in range(1, n)],
        out_specs=[spec(n + i) for i in range(len(shapes))],
        out_shape=[jax.ShapeDtypeStruct(shape, BF16) for shape in shapes],
        scratch_shapes=list(scratch),
        input_output_aliases=aliases or {},
        compiler_params=pltpu.CompilerParams(vmem_limit_bytes=mib * MIB),
        cost_estimate=cost and pl.CostEstimate(flops=cost, bytes_accessed=2_000_000, transcendentals=0),
        name=name,
    )(*inputs)


def edges_kernel(place, own, slab_a, slab_b, edge_a, edge_b, middle):
    even = place[1] == 0
    west, east = own[:REACH], own[COLS - REACH :]
    slab_a[...] = jnp.where(even, east, west)
    slab_b[...] = jnp.where(even, west, east)
    for slab, edge in ((slab_a, edge_a), (slab_b, edge_b)):
        block = turned(slab[...])
        edge[0], edge[1] = block[0], block[ROWS - 1]
    for b, left, n in chunks():
        block = turned_chunk(own[left : left + n])
        middle[0, left : left + 16] = block[0]
        middle[1, left : left + 16] = block[ROWS - 1]


def chunks():
    return [(b, 16 * b, min(16, COLS - 16 * b)) for b in range(PAD // 16)]


def fetches(source, target, sems):
    copies = [
        pltpu.make_async_copy(source.at[pl.ds(left, n)], target.at[pl.ds(left, n)], sems.at[b]) for b, left, n in chunks()
    ]
    for copy in copies:
        copy.start()
    return copies


def turned_chunk(block):
    if block.shape[0] < 16:
        block = jnp.concatenate([block, jnp.zeros((16 - block.shape[0], ROWS, CHANNELS), BF16)])
    return turned(block)


def ordered_kernel(place, middle, _, out):
    first = place[0] == 0
    out[0] = jnp.where(first, middle[1], middle[0])
    out[1] = jnp.where(first, middle[0], middle[1])


def widen_kernel(place, middle, got_a, got_b, wide_a, wide_b, joined):
    even, first = place[1] == 0, place[0] == 0
    left = jnp.where(even, got_b[...], got_a[...])
    right = jnp.where(even, got_a[...], got_b[...])
    for i, (wide, is_last) in enumerate(((wide_a, first), (wide_b, jnp.logical_not(first)))):
        pick = lambda x: jnp.where(is_last, x[1], x[0]).astype(F32)
        joined[i, :REACH] = pick(left)
        joined[i, REACH : REACH + PAD] = middle[i].astype(F32)
        joined[i, REACH + PAD :] = jnp.zeros((WIDE - REACH - PAD, CHANNELS), F32)
        joined[i, COLS + REACH : COLS + 2 * REACH] = pick(right)
        wide[...] = joined[i].astype(BF16)


LEAD = 8


def prepare_kernel(place, basis, reach, act, own, _, tiles, cells, rows, placed, buffer, sems):
    copies = fetches(act, buffer, sems)
    length = basis.shape[1] * FILTERS
    lats = basis.shape[3]
    offset = lax.broadcasted_iota(jnp.int32, (length, lats), 0) // FILTERS
    inside = jnp.abs(offset - REACH) <= reach[...]
    row = lax.broadcasted_iota(jnp.int32, (length, FILTERS * DEPTH), 0)
    col = lax.broadcasted_iota(jnp.int32, (length, FILTERS * DEPTH), 1)
    gap = jnp.where(row % FILTERS == col // DEPTH, col % DEPTH + row // FILTERS - 2 * REACH, -1)

    def put(t, q, lat):
        taps = jnp.where(inside, basis[t].astype(F32).reshape(length, lats), 0.0)[:, lat].astype(BF16)
        ones = jnp.where(gap == SPAN * q, 1.0, 0.0).astype(BF16)
        return lax.dot_general(taps, ones, (((0,), (0,)), ((), ())), preferred_element_type=F32)

    for q in range(TAPS):
        placed[q, LEAD : LEAD + lats, :] = put(TAPS - 1 - q, q, slice(None))
    placed[0, LEAD - 1 : LEAD, :] = put(0, 0, slice(0, 128))[:1]
    placed[2, LEAD + lats : LEAD + lats + 1, :] = put(2, 2, slice(lats - 128, lats))[127:]
    start = place[2] * ROWS + LEAD - 1
    for r in range(ROWS):
        for k in range(FILTERS):
            lanes = pl.ds(k * DEPTH, DEPTH)
            taps = [placed[q, pl.ds(start + r + q, 1), lanes] for q in range(TAPS)]
            band = jnp.broadcast_to(taps[0] + taps[1] + taps[2], (PART, DEPTH))
            band = pltpu.roll(band, SPAN * (r % 2), 1, stride=1, stride_axis=0)
            first = (r % 2) * FILTERS * PART + k * PART
            tiles[r // 2, first : first + PART, :] = band.astype(BF16)
    for b, left, n in chunks():
        copies[b].wait()
        cells[:, left : left + 16, :] = turned_chunk(buffer[left : left + n])
        rows[:, left : left + 16, :] = turned_chunk(own[left : left + n])


GROUP = 8
STEPS = ROWS // GROUP


def outer(f, cells):
    f = f.reshape(ROWS * PAD, CHANNELS)
    cells = cells.reshape(ROWS * PAD, CHANNELS)
    return lax.dot_general(f, cells, (((0,), (0,)), ((), ())), preferred_element_type=F32)


def stencil_kernel(place, tiles, rows, lon_b, lon_a, lat_a, lat_b, cells_ref, f_out, send, spans, joined, held, cells, sem, f_sems):
    step = pl.program_id(0)
    stores = [
        pltpu.make_async_copy(held.at[:, pl.ds(GROUP * i, GROUP)], f_out.at[:, pl.ds(GROUP * i, GROUP)], f_sems.at[i])
        for i in range(STEPS)
    ]
    copy = pltpu.make_async_copy(cells_ref, cells, sem)

    @pl.when(step == 0)
    def _():
        copy.start()
        even, first = place[1] == 0, place[0] == 0
        inner = slice(1, ROWS + 1)
        spans[0, inner, :REACH, :] = turned(jnp.where(even, lon_b[...], lon_a[...]))
        spans[0, inner, REACH:, :] = rows[:, :48, :]
        spans[1, inner, :, :] = rows[:, 16:80, :]
        spans[2, inner, :32, :] = rows[:, 48:80, :]
        joined[:, :16, :] = rows[:, 80:PAD, :].astype(F32)
        joined[:, 16:, :] = jnp.zeros((ROWS, 16, CHANNELS), F32)
        joined[:, COLS - 80 : COLS - 80 + REACH, :] = turned(jnp.where(even, lon_a[...], lon_b[...])).astype(F32)
        spans[2, inner, 32:, :] = joined[...].astype(BF16)
        before = jnp.where(first, lat_b[...], lat_a[...])
        after = jnp.where(first, lat_a[...], lat_b[...])
        for h in range(PARTS):
            spans[h, 0] = before[PART * h : PART * h + SPAN]
            spans[h, ROWS + 1] = after[PART * h : PART * h + SPAN]

    @pl.when(step < STEPS)
    def _():
        for pair in range(GROUP // 2):
            r = step * GROUP + 2 * pair
            for h in range(PARTS):
                taken = spans[h, pl.ds(r, 4)].reshape(DEPTH, CHANNELS)
                f = jnp.dot(tiles[pair], taken, preferred_element_type=F32).astype(BF16)
                f = f.reshape(2, FILTERS, PART, CHANNELS)
                for j in range(2):
                    held[:, r + j, h * PART : (h + 1) * PART, :] = f[j]

    for i, store in enumerate(stores):
        pl.when(step == i)(store.start)

    @pl.when(step == STEPS)
    def _():
        copy.wait()
        for j in range(2):
            send[j] = outer(held[2 * (1 - place[0]) + j], cells[...]).astype(BF16)
        for store in stores:
            store.wait()


def stencil(place, tiles, rows, lon_a, lon_b, lat_a, lat_b, cells):
    whole = lambda a: pl.BlockSpec(a.shape, lambda i, c: (0,) * a.ndim)
    return pl.pallas_call(
        stencil_kernel,
        grid_spec=pltpu.PrefetchScalarGridSpec(
            num_scalar_prefetch=1,
            grid=(STEPS + 1,),
            in_specs=[
                pl.BlockSpec((GROUP // 2, 2 * FILTERS * PART, DEPTH), lambda i, c: (jnp.minimum(i, STEPS - 1), 0, 0)),
                *[whole(a) for a in (rows, lon_b, lon_a, lat_a, lat_b)],
                pl.BlockSpec(memory_space=pl.ANY),
            ],
            out_specs=[
                pl.BlockSpec(memory_space=pltpu.HBM),
                pl.BlockSpec((2, CHANNELS, CHANNELS), lambda i, c: (0, 0, 0)),
            ],
            scratch_shapes=[
                pltpu.VMEM((PARTS, ROWS + 2, SPAN, CHANNELS), BF16),
                pltpu.VMEM((ROWS, 32, CHANNELS), F32),
                pltpu.VMEM((FILTERS, ROWS, PAD, CHANNELS), BF16),
                pltpu.VMEM((ROWS, PAD, CHANNELS), BF16),
                pltpu.SemaphoreType.DMA(()),
                pltpu.SemaphoreType.DMA((STEPS,)),
            ],
        ),
        out_shape=[
            jax.ShapeDtypeStruct((FILTERS, ROWS, PAD, CHANNELS), BF16),
            jax.ShapeDtypeStruct((2, CHANNELS, CHANNELS), BF16),
        ],
        compiler_params=pltpu.CompilerParams(vmem_limit_bytes=30 * MIB),
        name="stencil",
    )(place, tiles, rows, lon_b, lon_a, lat_a, lat_b, cells)


def own_part_kernel(place, f_hbm, cells_ref, mine, f, cells, sems):
    copies = [pltpu.make_async_copy(f_hbm.at[2 * place[0] + j], f.at[j], sems.at[j]) for j in range(2)]
    copies.append(pltpu.make_async_copy(cells_ref, cells, sems.at[2]))
    for copy in (copies[2], copies[0], copies[1]):
        copy.start()
    copies[2].wait()
    for j in range(2):
        copies[j].wait()
        mine[j] = outer(f[j], cells[...])


def spec(space):
    return pl.BlockSpec(memory_space=space)


def own_part(place, f, cells):
    return pl.pallas_call(
        own_part_kernel,
        in_specs=[spec(pltpu.SMEM), spec(pl.ANY), spec(pl.ANY)],
        out_specs=spec(pltpu.VMEM),
        out_shape=jax.ShapeDtypeStruct((2, CHANNELS, CHANNELS), F32),
        scratch_shapes=[
            pltpu.VMEM((2, ROWS, PAD, CHANNELS), BF16),
            pltpu.VMEM((ROWS, PAD, CHANNELS), BF16),
            pltpu.SemaphoreType.DMA((3,)),
        ],
        compiler_params=pltpu.CompilerParams(vmem_limit_bytes=16 * MIB),
        cost_estimate=pl.CostEstimate(flops=4 * ROWS * PAD * CHANNELS**2, bytes_accessed=6_000_000, transcendentals=0),
        name="own_part",
    )(place, f, cells)


SLAB = 32
SLABS = PAD // SLAB


def input_kernel(f_hbm, weight_hbm, out, weight, f, stage, weight_sems, f_sems, out_sems):
    loads = [pltpu.make_async_copy(weight_hbm.at[k], weight.at[k], weight_sems.at[k]) for k in range(FILTERS)]
    slabs = []
    for j in range(SLABS):
        at = pl.ds(SLAB * j, SLAB)
        slabs.append([pltpu.make_async_copy(f_hbm.at[k, :, at], f.at[k, :, at], f_sems.at[j, k]) for k in range(FILTERS)])
    for k in range(FILTERS):
        slabs[0][k].start()
        loads[k].start()
    for slab in slabs[1:]:
        for copy in slab:
            copy.start()
    stores = []
    for j in range(SLABS):
        left = SLAB * j
        cols = min(SLAB, COLS - left)
        total = 0.0
        for k in range(FILTERS):
            slabs[j][k].wait()
            if j == 0:
                loads[k].wait()
            taken = f[k, :, left : left + SLAB, :].reshape(ROWS * SLAB, CHANNELS)
            total += jnp.dot(taken, weight[k], preferred_element_type=F32)
        total = total.astype(BF16).reshape(ROWS, SLAB, CHANNELS)
        for b in range(SLAB // 16):
            stage[j, 16 * b : 16 * (b + 1)] = turned(total[:, 16 * b : 16 * (b + 1)])
        store = pltpu.make_async_copy(stage.at[j, pl.ds(0, cols)], out.at[pl.ds(left, cols)], out_sems.at[j])
        store.start()
        stores.append(store)
    for store in stores:
        store.wait()


def input_gradient(f, weight):
    flops = 2 * ROWS * PAD * FILTERS * CHANNELS * CHANNELS
    return pl.pallas_call(
        input_kernel,
        in_specs=[spec(pl.ANY), spec(pltpu.HBM)],
        out_specs=spec(pl.ANY),
        out_shape=jax.ShapeDtypeStruct((COLS, ROWS, CHANNELS), BF16),
        scratch_shapes=[
            pltpu.VMEM((FILTERS, CHANNELS, CHANNELS), BF16),
            pltpu.VMEM((FILTERS, ROWS, PAD, CHANNELS), BF16),
            pltpu.VMEM((SLABS, SLAB, ROWS, CHANNELS), BF16),
            pltpu.SemaphoreType.DMA((FILTERS,)),
            pltpu.SemaphoreType.DMA((SLABS, FILTERS)),
            pltpu.SemaphoreType.DMA((SLABS,)),
        ],
        compiler_params=pltpu.CompilerParams(vmem_limit_bytes=20 * MIB),
        cost_estimate=pl.CostEstimate(flops=flops, bytes_accessed=10_000_000, transcendentals=0),
        name="input_gradient",
    )(f, weight)


def put_half_kernel(flip, place, half, *rest):
    out, sems = rest[-2:]
    start = 2 * (1 - place[0] if flip else place[0])
    part = CHANNELS // 4
    copies = [
        pltpu.make_async_copy(half.at[:, pl.ds(i * part, part)], out.at[pl.ds(start, 2), pl.ds(i * part, part)], sems.at[i])
        for i in range(4)
    ]
    for copy in copies:
        copy.start()
    for copy in copies:
        copy.wait()


def put_half(place, half, flip, done=()):
    inputs = [place, half, *done]
    spaces = {i: pl.ANY for i in range(1, len(inputs) + 1)}
    return local(
        functools.partial(put_half_kernel, flip), "put_half", [(FILTERS, CHANNELS, CHANNELS)], inputs,
        [pltpu.SemaphoreType.DMA((4,))], spaces, {2: 0} if done else {},
    )


def device(lat, lon):
    return lat * LON + lon % LON


def route(target):
    return [(device(a, b), device(*target(a, b))) for a in range(LAT) for b in range(LON)]


def lat_b_partner(a, b):
    if a in (0, LAT - 1):
        return a, b + LON // 2
    return (a + 1 if a % 2 else a - 1), b


LON_A = route(lambda a, b: (a, b ^ 1))
LON_B = route(lambda a, b: (a, b + 1 if b % 2 else b - 1))
LAT_A = route(lambda a, b: (a ^ 1, b))
LAT_B = route(lat_b_partner)
SIBLING = LAT_A


def along_z(mask):
    return route(lambda a, b: (a, b ^ mask))


def haloes(own, place):
    slab, edge, wide = (REACH, ROWS, CHANNELS), (2, REACH, CHANNELS), (WIDE, CHANNELS)
    rows = (2, PAD, CHANNELS)
    slab_a, slab_b, edge_a, edge_b, middle = local(edges_kernel, "edges", [slab, slab, edge, edge, rows], [place, own])
    (middle,) = local(ordered_kernel, "ordered", [rows], [place, middle, edge_b], spaces={2: pl.ANY}, cost=4_000_000_000)
    edge_a = lax.ppermute(edge_a, AXES, LON_A)
    edge_b = lax.ppermute(edge_b, AXES, LON_B)
    lon_a = lax.ppermute(slab_a, AXES, LON_A)
    lon_b = lax.ppermute(slab_b, AXES, LON_B)
    wide_a, wide_b = local(
        widen_kernel, "widen", [wide, wide], [place, middle, edge_a, edge_b], [pltpu.VMEM((2, *wide), F32)]
    )
    return lon_a, lon_b, wide_a, wide_b


def prepared(place, basis, reach, act, own, after):
    lats = basis.shape[3]
    basis = jnp.transpose(basis, (1, 2, 0, 3))
    scratch = [
        pltpu.VMEM((TAPS, lats + 2 * LEAD, FILTERS * DEPTH), F32),
        pltpu.VMEM(act.shape, BF16),
        pltpu.SemaphoreType.DMA((PAD // 16,)),
    ]
    rows = (ROWS, PAD, CHANNELS)
    shapes = [(ROWS // 2, 2 * FILTERS * PART, DEPTH), rows, rows]
    inputs = [place, basis, reach.reshape(1, lats), act, own, after]
    return local(prepare_kernel, "prepare", shapes, inputs, scratch, {3: pltpu.HBM, 5: pl.ANY}, cost=1_000_000_000)


def summed(parts, groups, axes):
    parts = lax.all_to_all(parts.reshape(groups, -1, CHANNELS), axes, 0, 0, tiled=True)
    return jnp.sum(parts.astype(F32), axis=0)


def on_device(cotangent, activations, weight, basis, reach):
    band = lax.axis_index(("y", "xh", "core")).astype(jnp.int32)
    core = lax.axis_index("core").astype(jnp.int32)
    odd = lax.axis_index("zl").astype(jnp.int32)
    place = jnp.stack([core, odd, band])
    own, act = jnp.swapaxes(cotangent, 0, 1), jnp.swapaxes(activations, 0, 1)
    act = pltpu.with_memory_space_constraint(act, pltpu.HBM)
    lon_a, lon_b, wide_a, wide_b = haloes(own, place)
    lat_a = lax.ppermute(wide_a, AXES, LAT_A)
    lat_b = lax.ppermute(wide_b, AXES, LAT_B)
    tiles, cells, rows = prepared(place, basis, reach, act, own, wide_a)
    f, send = stencil(place, tiles, rows, lon_a, lon_b, lat_a, lat_b, cells)
    got = lax.ppermute(send, AXES, SIBLING)
    mine = own_part(place, f, cells)
    half = (mine + got.astype(F32)).astype(BF16)
    weight = pltpu.with_memory_space_constraint(weight, pltpu.HBM)
    grad_input = input_gradient(f, weight)
    part = summed(half.reshape(-1, CHANNELS), 32, BLOCK).astype(BF16)
    part, grad_input = lax.optimization_barrier((part, grad_input))
    others = [lax.ppermute(part, AXES, along_z(m)).astype(F32) for m in (2, 6, 4)]
    norm_factor = float(ROWS * COLS * LAT * LON) ** (-0.5)
    part = (part.astype(F32) + others[0]) + (others[1] + others[2])
    part = (part * norm_factor).astype(BF16)
    parts = lax.all_to_all(jnp.broadcast_to(part, (32, *part.shape)), BLOCK, 0, 0, tiled=True)
    mine = parts.reshape(2, CHANNELS, CHANNELS)
    theirs = lax.ppermute(mine, AXES, SIBLING)
    grad_weight = put_half(place, mine, False)
    (grad_weight,) = put_half(place, theirs, True, grad_weight)
    return jnp.swapaxes(grad_input, 0, 1), grad_weight


def solution(mesh):
    finer = Mesh(mesh.devices.reshape(4, 2, 2, 2, 4, 2), AXES)
    cells = P(("y", "xh", "core"), ("xl", "zh", "zl"), None)
    return jax.shard_map(
        on_device, mesh=finer, in_specs=(cells, cells, P(), P(), P()), out_specs=(cells, P()), check_vma=False
    )
```
